256 devices in a mesh: row: 8 (over z), col: 8 (over y, core), layer: 4 (over x).
Axes of the slice: x: 4, y: 4, z: 8, core: 2. Of those that a mesh axis runs over, the one named last changes fastest.
Arguments:
- density: bfloat16 [1280, 8, 4, 2, 128, 128], P('row', 'col', 'layer'), may hold values from -0.375 to 0.375
- band_length: int32 [1280], replicated, may hold values from 4 to 64, as said below
- band_start: int32 [1280], replicated, may hold values from -63 to 0, as said below
Outputs:
- purified: float32 [64, 8, 4, 2, 128, 128], P('row', 'col', 'layer')
The draws below stay inside these ranges and needn't reach their ends.
Inputs may be any that keep to these rules, and one draw needn't show every extreme that they name: `band_length`: rows of every device's range of 1280 // 8 rows reach 64 blocks; every window row has 64 blocks. band_start[i] is at least 1 - band_length[i], so each row's run of columns covers its diagonal block; every window row has band_start = -32.
All inputs are finite; a program needn't handle non-finite values.
Results may differ from the reference program's by a relative error of at most 0.0029.
Values may be sent and summed in bfloat16 or wider, within the bound.
A program may use at most 192 MiB of HBM per device.

```python
import jax
import jax.numpy as jnp
from jax import lax

BS = 128
NB = 1280
KMAX = 64
KMIN = 4
NR = 64
STRIDE = 20
EA = 2
N_COL = 8
N_LAYER = 4


def window_flags():
    positions = jnp.arange(NB, dtype=jnp.int32)
    spacing = NB // NR
    return positions % spacing == spacing // 2


def band_lengths(key):
    group_count = NB // 8
    lengths = jax.random.randint(key, (NB,), KMIN, KMAX + 1)
    picked = jax.random.randint(jax.random.fold_in(key, 11), (group_count,), 0, 8)
    positions = jnp.arange(NB, dtype=jnp.int32)
    chosen = jnp.repeat(picked, 8)
    lengths = jnp.where(positions % 8 == chosen, KMAX, lengths)
    return jnp.where(window_flags(), KMAX, lengths).astype(jnp.int32)


def draw_band_length(key, part):
    lengths = band_lengths(key)
    return lengths


def draw_band_start(key, part):
    lengths = band_lengths(key)
    key = jax.random.fold_in(key, 2)
    spread = jax.random.randint(key, (NB,), 0, KMAX)
    starts = -(spread % lengths)
    return jnp.where(window_flags(), -(KMAX // 2), starts).astype(jnp.int32)


def levels(stream_key, dims, pieces, smallest, top_value):
    def one(dim, shards_of):
        draws = jax.random.uniform(jax.random.fold_in(jax.random.fold_in(stream_key, 6), dim), (shards_of,), jnp.float32, smallest / len(pieces), top_value / len(pieces))
        return jnp.repeat(jnp.exp(draws), dims[dim] // shards_of).reshape((-1,) + (1,) * (len(dims) - dim - 1))

    factor_of = one(*pieces[0])
    for cut in pieces[1:]:
        factor_of = factor_of * one(*cut)
    return factor_of


def scatter_about(rng, shape, scale, bound, cuts=(), held_as=jnp.bfloat16):
    entries = jax.random.normal(rng, shape, jnp.float32) * scale
    if len(cuts) > 0:
        entries = levels(rng, shape, cuts, -0.22, 0.18) * entries
    return jnp.clip(entries, min=-bound, max=bound).astype(held_as)


def setup_inputs(seed: int = 0) -> dict:
    key_of = jax.random.split(jax.random.key(seed), 4)
    density = scatter_about(key_of[0], (NB, N_COL, N_LAYER, EA, BS, BS), 0.06, 0.375, ((0, 8), (1, 8), (2, 4)))
    band_length = draw_band_length(jax.random.fold_in(key_of[3], 71), 0)
    band_start = draw_band_start(jax.random.fold_in(key_of[3], 71), 0)
    return dict(density=density, band_length=band_length, band_start=band_start)


def slot_columns(block_rows, run_start, run_length, residue, slot_ids, cell_count, order_size):
    offset = jnp.mod(residue - block_rows - run_start, cell_count) + slot_ids * cell_count
    return jnp.mod(block_rows + run_start + offset, order_size), offset < run_length


def reference(density, band_length, band_start):
    cell_count = N_COL * N_LAYER
    col_ids = jnp.arange(N_COL, dtype=jnp.int32)
    layer_ids = jnp.arange(N_LAYER, dtype=jnp.int32)
    residues = layer_ids[None, :] * N_COL + col_ids[:, None]
    slot_ids = jnp.arange(EA, dtype=jnp.int32)
    all_rows = jnp.arange(NB, dtype=jnp.int32)
    columns, live = slot_columns(all_rows[:, None, None, None], band_start[:, None, None, None],
                                 band_length[:, None, None, None], residues[None, :, :, None],
                                 slot_ids[None, None, None, :], cell_count, NB)
    window_rows = (jnp.arange(NR, dtype=jnp.int32) * STRIDE + STRIDE // 2).astype(jnp.int32)
    window_cols = columns[window_rows]
    window_live = live[window_rows]
    slot_total = N_COL * N_LAYER * EA

    def product(panel):
        def one_row(inputs):
            left_blocks, row_cols, row_live = inputs
            inner_flat = row_cols.reshape(slot_total)
            live_flat = row_live.reshape(slot_total)
            source = columns[inner_flat]
            source_live = live[inner_flat]
            matches = ((source[:, :, :, None, :] == row_cols[None, :, :, :, None])
                       & source_live[:, :, :, None, :] & row_live[None, :, :, :, None]
                       & live_flat[:, None, None, None, None])
            right_blocks = density[inner_flat].astype(jnp.float32)
            selected = jnp.einsum("sclfe,sclexy->sclfxy", matches.astype(jnp.float32), right_blocks)
            left_flat = left_blocks.reshape(slot_total, BS, BS).astype(jnp.float32)
            return jnp.einsum("sxz,sclfzy->clfxy", left_flat, selected)
        return lax.map(one_row, (panel, window_cols, window_live))

    square_part = product(density[window_rows]).astype(jnp.bfloat16)
    cube_part = product(square_part)
    return 3.0 * square_part.astype(jnp.float32) - 2.0 * cube_part
```

```python
import jax
import jax.numpy as jnp
from jax import lax
from jax.experimental import pallas as pl
from jax.experimental.pallas import tpu as pltpu
from jax.sharding import PartitionSpec as P

BS = 128
NB = 1280
SPAN = 160
STRIDE = 20
EA = 2
CELLS = 32
ITEMS = 4
BANK = 124
HALO = 22
MESH = pl.DeviceIdType.MESH


def wrap4(v):
    return lax.rem(v + 8, 4)


def purify(
    density, length, start, out,
    bank, panel, acc, stage,
    ring_send, ring_recv, own_sem, mate_send, mate_recv,
    bank_sem, bank_send, bank_recv, halo_send, halo_recv,
    out_sem, out_send, out_recv,
):
    z = lax.axis_index("row")
    col = lax.axis_index("col")
    x = lax.axis_index("layer")
    y = col // 2
    h = lax.rem(col, 2)
    p = 1 - h

    def at(dx=0, dy=0):
        return (z, wrap4(y + dy) * 2 + h, wrap4(x + dx))

    mate = (z, y * 2 + p, x)
    up = lax.rem(z + 1, 8)
    down = lax.rem(z + 7, 8)
    source_z = lax.rem(z + 7 + 2 * h, 8)
    barrier = pltpu.get_barrier_semaphore()
    for other in (
        at(dx=1), at(dx=-1), at(dy=1), at(dy=-1), mate,
        (source_z, y * 2, x), (source_z, y * 2 + 1, x),
    ):
        pl.semaphore_signal(barrier, inc=1, device_id=other, device_id_type=MESH)
    pl.semaphore_wait(barrier, 7)

    place = ((y, x), (x, y))
    outer_h = y + h * (x - y)
    inner_h = x + h * (y - x)

    def window_of(i, core):
        return 3 + core + i * (2 * core - 1)

    def own_copy(i):
        row = STRIDE // 2 + STRIDE * window_of(i, h)
        return pltpu.make_async_copy(
            density.at[row], panel.at[i, h, :, outer_h, inner_h], own_sem.at[i]
        )

    def mate_copy(i):
        row = STRIDE // 2 + STRIDE * window_of(i, p)
        return pltpu.make_async_remote_copy(
            src_ref=density.at[row],
            dst_ref=panel.at[i, h, :, outer_h, inner_h],
            send_sem=mate_send.at[i],
            recv_sem=mate_recv.at[i],
            device_id=mate,
            device_id_type=MESH,
        )

    def mate_arrival(i):
        outer_p = y + p * (x - y)
        inner_p = x + p * (y - x)
        here = panel.at[i, p, :, outer_p, inner_p]
        return pltpu.make_async_remote_copy(
            src_ref=here, dst_ref=here, send_sem=mate_send.at[i], recv_sem=mate_recv.at[i],
            device_id=mate, device_id_type=MESH,
        )

    for i in range(ITEMS):
        mate_copy(i).start()
        own_copy(i).start()

    def bank_piece(piece, core):
        if piece == 0:
            return 64, 38 + 20 * core, 60 - 60 * core
        if piece == 1:
            return 20, 18 + 104 * core, 40 + 24 * core
        return 18, 142 * core, 22 + 62 * core

    def bank_own(piece):
        size, src, dst = bank_piece(piece, h)
        return pltpu.make_async_copy(
            density.at[pl.ds(src, size)], bank.at[h, pl.ds(dst, size)], bank_sem.at[piece]
        )

    def bank_mate(piece):
        size, src, dst = bank_piece(piece, p)
        return pltpu.make_async_remote_copy(
            src_ref=density.at[pl.ds(src, size)],
            dst_ref=bank.at[h, pl.ds(dst, size)],
            send_sem=bank_send.at[piece],
            recv_sem=bank_recv.at[piece],
            device_id=mate,
            device_id_type=MESH,
        )

    def bank_arrival(piece):
        size, _, dst = bank_piece(piece, h)
        here = bank.at[p, pl.ds(dst, size)]
        return pltpu.make_async_remote_copy(
            src_ref=here, dst_ref=here, send_sem=bank_send.at[piece], recv_sem=bank_recv.at[piece],
            device_id=mate, device_id_type=MESH,
        )

    def halo_copy(piece, side):
        size = (2, 20)[piece]
        src = ((SPAN - 2, SPAN - 22), (0, 2))[side][piece]
        dst = ((20, 0), (102, 104))[side][piece]
        return pltpu.make_async_remote_copy(
            src_ref=density.at[pl.ds(src, size)],
            dst_ref=bank.at[h, pl.ds(dst, size)],
            send_sem=halo_send.at[piece, side],
            recv_sem=halo_recv.at[piece, h],
            device_id=((up, y * 2, x), (down, y * 2 + 1, x))[side],
            device_id_type=MESH,
        )

    def halo_arrival(piece, cell):
        size = (2, 20)[piece]
        dst = (20 + 82 * h, 104 * h)[piece]
        here = bank.at[cell, pl.ds(dst, size)]
        return pltpu.make_async_remote_copy(
            src_ref=here, dst_ref=here,
            send_sem=halo_send.at[piece, 0], recv_sem=halo_recv.at[piece, cell],
            device_id=mate, device_id_type=MESH,
        )

    for piece in range(2):
        for side in range(2):
            halo_copy(piece, side).start()
    for piece in range(3):
        bank_mate(piece).start()
        bank_own(piece).start()

    def target(g, step, way):
        move = 1 - 2 * way
        if (g == 0) == (step < 2):
            return at(dx=move)
        return at(dy=move)

    def region(i, g, step, way, arriving):
        outer, inner = place[g]
        back = (2 * way - 1) * ((step % 2) + (1 if arriving else 0))
        if step == 0:
            return panel.at[i, g, :, outer, wrap4(inner + back)]
        if step == 1:
            return panel.at[i, g, way, outer, wrap4(inner + back)]
        if step == 2:
            return panel.at[i, g, :, wrap4(outer + back)]
        return panel.at[i, g, way, wrap4(outer + back)]

    def ring(i, g, step, way, arriving=False):
        here = region(i, g, step, way, arriving)
        return pltpu.make_async_remote_copy(
            src_ref=here,
            dst_ref=here,
            send_sem=ring_send.at[i, g, step, way],
            recv_sem=ring_recv.at[i, g, step, way],
            device_id=target(g, step, way),
            device_id_type=MESH,
        )

    def send(i, step):
        for g in range(2):
            for way in range(2):
                ring(i, g, step, way).start()

    def arrive(i, step):
        for g in range(2):
            for way in range(2):
                ring(i, g, step, way, arriving=True).wait_recv()

    def sent(i):
        for g in range(2):
            for step in range(4):
                for way in range(2):
                    ring(i, g, step, way).wait_send()

    def advance(i, step):
        arrive(i, step - 1)
        send(i, step)

    for i in range(ITEMS):
        own_copy(i).wait()
        mate_arrival(i).wait_recv()
        send(i, 0)
    for i in range(ITEMS):
        advance(i, 1)
    advance(0, 2)
    advance(1, 2)
    advance(0, 3)

    def slab(i, slot, window, j):
        g = lax.rem(j, 2)
        outer = wrap4(y + g * (x - y) + j // 2 - 1)
        anchor = STRIDE // 2 + STRIDE * window
        bank0 = STRIDE * (window - 4 * h)
        row0 = SPAN * z + anchor + NB - 32
        places = [
            lax.rem(8 * x + 2 * y + cell + 256 - anchor, CELLS) for cell in range(2)
        ]
        left, right = [], []
        for inner in range(4):
            residue = 8 * inner + 2 * outer + g * (6 * outer - 6 * inner + 1)
            base = lax.rem(residue + 256 - anchor, CELLS)
            for e in range(EA):
                t = base + CELLS * e
                k = lax.rem(row0 + t, NB)
                run_start = start[k]
                run_length = length[k]
                pieces = []
                for cell in range(2):
                    s0 = bank[cell, bank0 + t, 0]
                    s1 = bank[cell, bank0 + t, 1]
                    for f in range(EA):
                        at_run = places[cell] + CELLS * f - t - run_start
                        live = (at_run >= 0) & (at_run < run_length)
                        code = jnp.where(live, jnp.where(at_run < CELLS, 1, 2), 0)
                        pieces.append(
                            jnp.where(code == 1, s0, jnp.where(code == 2, s1, jnp.zeros_like(s1)))
                        )
                right.append(jnp.concatenate(pieces, axis=1))
                left.append(panel[i, g, e, outer, inner])
        acc[...] += jnp.dot(
            jnp.concatenate(left, axis=1),
            jnp.concatenate(right, axis=0),
            preferred_element_type=jnp.float32,
        )

    def out_own(slot):
        return pltpu.make_async_copy(
            stage.at[slot, h], out.at[window_of(slot, h)], out_sem.at[slot]
        )

    def out_mate(slot):
        return pltpu.make_async_remote_copy(
            src_ref=stage.at[slot, p],
            dst_ref=out.at[window_of(slot, h)],
            send_sem=out_send.at[slot],
            recv_sem=out_recv.at[slot],
            device_id=mate,
            device_id_type=MESH,
        )

    def out_arrival(slot):
        here = out.at[window_of(slot, p)]
        return pltpu.make_async_remote_copy(
            src_ref=here, dst_ref=here, send_sem=out_send.at[slot], recv_sem=out_recv.at[slot],
            device_id=mate, device_id_type=MESH,
        )

    def item(i, _):
        slot = lax.rem(i, ITEMS)
        window = window_of(slot, h)

        @pl.when((i >= 1) & (i < 5))
        def _():
            advance(i + 3, 1)

        @pl.when(i < 6)
        def _():
            advance(i + 2, 2)

        @pl.when(i == 0)
        def _():
            bank_own(0).wait()
            bank_arrival(0).wait_recv()

        @pl.when(i == 1)
        def _():
            bank_own(1).wait()
            bank_arrival(1).wait_recv()

        @pl.when(i == 2)
        def _():
            bank_own(2).wait()
            bank_arrival(2).wait_recv()
            halo_arrival(0, 0).wait_recv()
            halo_arrival(0, 1).wait_recv()

        @pl.when(i == 3)
        def _():
            halo_arrival(1, 0).wait_recv()
            halo_arrival(1, 1).wait_recv()

        acc[...] = jnp.zeros_like(acc)

        def body(j, _):
            slab(i, slot, window, j)
            return 0

        lax.fori_loop(0, 6, body, 0)
        arrive(i, 3)

        @pl.when(i < 7)
        def _():
            advance(i + 1, 3)

        lax.fori_loop(6, 8, body, 0)

        @pl.when(i < 4)
        def _():
            for cell in range(2):
                outer, inner = place[cell]
                for f in range(EA):
                    lo = (cell * EA + f) * BS
                    panel[i + 4, cell, f, outer, inner] = acc[:, lo : lo + BS].astype(jnp.bfloat16)
            send(i + 4, 0)

        @pl.when(i >= 4)
        def _():
            for cell in range(2):
                outer, inner = place[cell]
                for f in range(EA):
                    lo = (cell * EA + f) * BS
                    square = panel[i, cell, f, outer, inner].astype(jnp.float32)
                    stage[slot, cell, f] = 3.0 * square - 2.0 * acc[:, lo : lo + BS]
            out_mate(slot).start()
            out_own(slot).start()

        @pl.when(i >= 2)
        def _():
            sent(i - 2)

        return 0

    lax.fori_loop(0, 2 * ITEMS, item, 0)

    sent(6)
    sent(7)
    for i in range(ITEMS):
        mate_copy(i).wait_send()
    for piece in range(3):
        bank_mate(piece).wait_send()
    for piece in range(2):
        for side in range(2):
            halo_copy(piece, side).wait_send()
    for slot in range(ITEMS):
        out_own(slot).wait()
        out_mate(slot).wait_send()
        out_arrival(slot).wait_recv()


def shards(density, band_length, band_start):
    dma = pltpu.SemaphoreType.DMA
    result = pl.pallas_call(
        purify,
        out_shape=jax.ShapeDtypeStruct((2 * ITEMS, EA, BS, BS), jnp.float32),
        in_specs=[
            pl.BlockSpec(memory_space=pl.ANY),
            pl.BlockSpec(memory_space=pltpu.SMEM),
            pl.BlockSpec(memory_space=pltpu.SMEM),
        ],
        out_specs=pl.BlockSpec(memory_space=pl.ANY),
        scratch_shapes=[
            pltpu.VMEM((2, BANK, EA, BS, BS), jnp.bfloat16),
            pltpu.VMEM((2 * ITEMS, 2, EA, 4, 4, BS, BS), jnp.bfloat16),
            pltpu.VMEM((BS, 4 * BS), jnp.float32),
            pltpu.VMEM((ITEMS, 2, EA, BS, BS), jnp.float32),
            dma((2 * ITEMS, 2, 4, 2)), dma((2 * ITEMS, 2, 4, 2)),
            dma((ITEMS,)), dma((ITEMS,)), dma((ITEMS,)),
            dma((3,)), dma((3,)), dma((3,)),
            dma((2, 2)), dma((2, 2)),
            dma((ITEMS,)), dma((ITEMS,)), dma((ITEMS,)),
        ],
        compiler_params=pltpu.CompilerParams(
            collective_id=0, has_side_effects=True, vmem_limit_bytes=48 * 2**20
        ),
        name="purify",
    )(density.reshape(SPAN, EA, BS, BS), band_length, band_start)
    return result.reshape(2 * ITEMS, 1, 1, EA, BS, BS)


def solution(mesh):
    in_specs = (P("row", "col", "layer", None, None, None), P(), P())
    out_specs = P("row", "col", "layer", None, None, None)
    return jax.shard_map(shards, mesh=mesh, in_specs=in_specs, out_specs=out_specs, check_vma=False)
```

```python
import jax
import jax.numpy as jnp
from jax import lax
from jax.experimental import pallas as pl
from jax.experimental.pallas import tpu as pltpu
from jax.sharding import PartitionSpec as P

BS = 128
NB = 1280
SPAN = 160
STRIDE = 20
EA = 2
CELLS = 32
ITEMS = 4
BANK = 124
HALO = 22
MESH = pl.DeviceIdType.MESH


def wrap4(v):
    return lax.rem(v + 8, 4)


def purify(
    rows, density, length_in, start_in, out,
    bank, panel, acc, stage, length, start, band_sem,
    first_send, first_recv, ring_send, ring_recv, own_sem, mate_send, mate_recv,
    bank_sem, bank_send, bank_recv, halo_send, halo_recv,
    out_sem, out_send, out_recv,
):
    z = lax.axis_index("row")
    col = lax.axis_index("col")
    x = lax.axis_index("layer")
    y = col // 2
    h = lax.rem(col, 2)
    p = 1 - h

    def at(dx=0, dy=0):
        return (z, wrap4(y + dy) * 2 + h, wrap4(x + dx))

    mate = (z, y * 2 + p, x)
    up = lax.rem(z + 1, 8)
    down = lax.rem(z + 7, 8)
    source_z = lax.rem(z + 7 + 2 * h, 8)
    barrier = pltpu.get_barrier_semaphore()
    for other in (
        at(dx=1), at(dx=-1), at(dy=1), at(dy=-1), mate,
        (source_z, y * 2, x), (source_z, y * 2 + 1, x),
    ):
        pl.semaphore_signal(barrier, inc=1, device_id=other, device_id_type=MESH)
    pl.semaphore_wait(barrier, 7)

    place = ((y, x), (x, y))

    def local_of(i, core):
        return 3 - 3 * core + i * (2 * core - 1)

    def panel_of(i):
        slot = lax.rem(i, ITEMS)
        return i - slot + local_of(slot, h)

    def blocks_of(count):
        return bank.at[0, pl.ds(0, count // EA)]

    def take(sem, count, sending=False):
        here = blocks_of(count)
        copy = pltpu.make_async_remote_copy(
            src_ref=here, dst_ref=here, send_sem=sem, recv_sem=sem,
            device_id=mate, device_id_type=MESH,
        )
        if sending:
            copy.wait_send()
        else:
            copy.wait_recv()

    def half_of(half, core):
        return 2 - 2 * core + half * (4 * core - 2)

    def own_copy(g):
        outer, inner = place[g]
        return pltpu.make_async_copy(
            density.at[pl.ds(4 * h, 4), STRIDE // 2, g],
            panel.at[pl.ds(0, 4), g, h, outer, inner],
            own_sem.at[g],
        )

    def mate_copy(half, g):
        outer, inner = place[g]
        low = half_of(half, p)
        return pltpu.make_async_remote_copy(
            src_ref=density.at[pl.ds(4 * p + low, 2), STRIDE // 2, g],
            dst_ref=panel.at[pl.ds(low, 2), g, h, outer, inner],
            send_sem=mate_send.at[half, g],
            recv_sem=mate_recv.at[half, g],
            device_id=mate,
            device_id_type=MESH,
        )

    def mate_arrival(half, g):
        outer, inner = place[g]
        here = panel.at[pl.ds(half_of(half, h), 2), g, p, outer, inner]
        return pltpu.make_async_remote_copy(
            src_ref=here, dst_ref=here,
            send_sem=mate_send.at[half, g], recv_sem=mate_recv.at[half, g],
            device_id=mate, device_id_type=MESH,
        )

    def target(g, step, way):
        move = 1 - 2 * way
        if (g == 0) == (step < 2):
            return at(dx=move)
        return at(dy=move)

    def push(src, dst, send_sem, recv_sem, g, step, way):
        pltpu.make_async_remote_copy(
            src_ref=src, dst_ref=dst, send_sem=send_sem, recv_sem=recv_sem,
            device_id=target(g, step, way), device_id_type=MESH,
        ).start()

    def first_own(half):
        low = half_of(half, h)
        for g in range(2):
            outer, inner = place[g]
            for way in range(2):
                push(
                    density.at[pl.ds(4 * h + low, 2), STRIDE // 2, g],
                    panel.at[pl.ds(low, 2), g, h, outer, inner],
                    first_send.at[half], first_recv.at[half, 0], g, 0, way,
                )

    def first_mate(half):
        low = half_of(half, h)
        for g in range(2):
            outer, inner = place[g]
            mate_arrival(half, g).wait_recv()
            here = panel.at[pl.ds(low, 2), g, p, outer, inner]
            for way in range(2):
                push(here, here, first_send.at[half], first_recv.at[half, 0], g, 0, way)

    def first_forward(half):
        low = half_of(half, h)
        take(first_recv.at[half, 0], 16)
        for g in range(2):
            outer, inner = place[g]
            for way in range(2):
                here = panel.at[pl.ds(low, 2), g, way, outer, wrap4(inner + 2 * way - 1)]
                push(here, here, first_send.at[half], first_recv.at[half, 1], g, 1, way)

    def send(i, step):
        n = panel_of(i)
        for g in range(2):
            outer, inner = place[g]
            for way in range(2):
                back = 2 * way - 1
                if step == 0:
                    here = panel.at[n, g, :, outer, inner]
                elif step == 1:
                    here = panel.at[n, g, way, outer, wrap4(inner + back)]
                elif step == 2:
                    here = panel.at[n, g, :, outer]
                else:
                    here = panel.at[n, g, way, wrap4(outer + back)]
                push(here, here, ring_send.at[i], ring_recv.at[i, step], g, step, way)

    arriving = (8, 4, 32, 16)

    def arrive(i, step):
        take(ring_recv.at[i, step], arriving[step])

    def forward(i, step):
        arrive(i, step - 1)
        send(i, step)

    for half in range(2):
        for g in range(2):
            mate_copy(half, g).start()
        first_own(half)
    for g in range(2):
        own_copy(g).start()
    pltpu.make_async_copy(length_in, length, band_sem.at[0]).start()
    pltpu.make_async_copy(start_in, start, band_sem.at[1]).start()
    for half in range(2):
        first_mate(half)

    def bank_piece(piece, core):
        if piece == 0:
            return 64, 38 + 20 * core, 60 - 60 * core
        if piece == 1:
            return 20, 18 + 104 * core, 40 + 24 * core
        return 18, 142 * core, 22 + 62 * core

    def bank_own(piece):
        size, src, dst = bank_piece(piece, h)
        return pltpu.make_async_copy(
            rows.at[pl.ds(src, size)], bank.at[h, pl.ds(dst, size)], bank_sem.at[piece]
        )

    def bank_mate(piece):
        size, src, dst = bank_piece(piece, p)
        return pltpu.make_async_remote_copy(
            src_ref=rows.at[pl.ds(src, size)],
            dst_ref=bank.at[h, pl.ds(dst, size)],
            send_sem=bank_send.at[piece],
            recv_sem=bank_recv.at[piece],
            device_id=mate,
            device_id_type=MESH,
        )

    def bank_arrival(piece):
        size, _, dst = bank_piece(piece, h)
        here = bank.at[p, pl.ds(dst, size)]
        return pltpu.make_async_remote_copy(
            src_ref=here, dst_ref=here, send_sem=bank_send.at[piece], recv_sem=bank_recv.at[piece],
            device_id=mate, device_id_type=MESH,
        )

    def halo_copy(piece, side):
        size = (2, 20)[piece]
        src = ((SPAN - 2, SPAN - 22), (0, 2))[side][piece]
        dst = ((20, 0), (102, 104))[side][piece]
        return pltpu.make_async_remote_copy(
            src_ref=rows.at[pl.ds(src, size)],
            dst_ref=bank.at[h, pl.ds(dst, size)],
            send_sem=halo_send.at[piece, side],
            recv_sem=halo_recv.at[piece, h],
            device_id=((up, y * 2, x), (down, y * 2 + 1, x))[side],
            device_id_type=MESH,
        )

    def halo_arrival(piece, cell):
        size = (2, 20)[piece]
        dst = (20 + 82 * h, 104 * h)[piece]
        here = bank.at[cell, pl.ds(dst, size)]
        return pltpu.make_async_remote_copy(
            src_ref=here, dst_ref=here,
            send_sem=halo_send.at[piece, 0], recv_sem=halo_recv.at[piece, cell],
            device_id=mate, device_id_type=MESH,
        )

    for piece in range(2):
        for side in range(2):
            halo_copy(piece, side).start()
    for piece in range(3):
        bank_mate(piece).start()
        bank_own(piece).start()

    first_forward(0)
    first_forward(1)
    own_copy(0).wait()
    own_copy(1).wait()
    take(first_recv.at[0, 1], 8)
    send(0, 2)
    send(1, 2)
    pltpu.make_async_copy(length_in, length, band_sem.at[0]).wait()
    pltpu.make_async_copy(start_in, start, band_sem.at[1]).wait()
    forward(0, 3)
    take(first_recv.at[1, 1], 8)

    def slab(n, local, j):
        g = lax.rem(j, 2)
        outer = wrap4(y + g * (x - y) + j // 2 - 1)
        anchor = STRIDE // 2 + STRIDE * (4 * h + local)
        bank0 = STRIDE * local
        row0 = SPAN * z + anchor - 32
        places = [
            lax.rem(8 * x + 2 * y + cell + 256 - anchor, CELLS) for cell in range(2)
        ]
        left, right = [], []
        for inner in range(4):
            residue = 8 * inner + 2 * outer + g * (6 * outer - 6 * inner)
            for place_cell in range(2):
                t = lax.rem(residue + place_cell + 256 - anchor, CELLS) + CELLS * g
                k = row0 + t
                k = jnp.where(k < 0, k + NB, jnp.where(k >= NB, k - NB, k))
                run_start = start[k]
                run_length = length[k]
                pieces = []
                for cell in range(2):
                    s0 = bank[cell, bank0 + t, 0]
                    s1 = bank[cell, bank0 + t, 1]
                    for f in range(EA):
                        at_run = places[cell] + CELLS * f - t - run_start
                        live = (at_run >= 0) & (at_run < run_length)
                        code = jnp.where(live, jnp.where(at_run < CELLS, 1, 2), 0)
                        pieces.append(
                            jnp.where(code == 1, s0, jnp.where(code == 2, s1, jnp.zeros_like(s1)))
                        )
                right.append(jnp.concatenate(pieces, axis=1))
                left.append(panel[n, g, place_cell, outer, inner])
        acc[...] += jnp.dot(
            jnp.concatenate(left, axis=1),
            jnp.concatenate(right, axis=0),
            preferred_element_type=jnp.float32,
        )

    def out_own(slot):
        return pltpu.make_async_copy(
            stage.at[slot, h], out.at[4 * h + local_of(slot, h)], out_sem.at[slot]
        )

    def out_mate(slot):
        return pltpu.make_async_remote_copy(
            src_ref=stage.at[slot, p],
            dst_ref=out.at[4 * h + local_of(slot, h)],
            send_sem=out_send.at[slot],
            recv_sem=out_recv.at[slot],
            device_id=mate,
            device_id_type=MESH,
        )

    def out_arrival(slot):
        here = out.at[4 * p + local_of(slot, p)]
        return pltpu.make_async_remote_copy(
            src_ref=here, dst_ref=here, send_sem=out_send.at[slot], recv_sem=out_recv.at[slot],
            device_id=mate, device_id_type=MESH,
        )

    def item(i, _):
        slot = lax.rem(i, ITEMS)
        local = local_of(slot, h)
        n = panel_of(i)

        @pl.when(i < 2)
        def _():
            send(i + 2, 2)

        @pl.when((i >= 2) & (i < 6))
        def _():
            forward(i + 2, 2)

        @pl.when((i >= 1) & (i < 5))
        def _():
            forward(i + 3, 1)

        @pl.when(i == 0)
        def _():
            bank_own(0).wait()
            bank_arrival(0).wait_recv()

        @pl.when(i == 1)
        def _():
            bank_own(1).wait()
            bank_arrival(1).wait_recv()

        @pl.when(i == 2)
        def _():
            bank_own(2).wait()
            bank_arrival(2).wait_recv()
            halo_arrival(0, 0).wait_recv()
            halo_arrival(0, 1).wait_recv()

        @pl.when(i == 3)
        def _():
            halo_arrival(1, 0).wait_recv()
            halo_arrival(1, 1).wait_recv()

        @pl.when(i == 5)
        def _():
            for half in range(2):
                take(first_send.at[half], 24, sending=True)
                for g in range(2):
                    mate_copy(half, g).wait_send()
            for m in range(ITEMS):
                take(ring_send.at[m], 48, sending=True)
            for piece in range(3):
                bank_mate(piece).wait_send()
            for piece in range(2):
                for side in range(2):
                    halo_copy(piece, side).wait_send()

        @pl.when(i >= 5)
        def _():
            out_own(slot - 1).wait()
            out_mate(slot - 1).wait_send()
            out_arrival(slot - 1).wait_recv()

        acc[...] = jnp.zeros_like(acc)

        def body(j, _):
            slab(n, local, j)
            return 0

        lax.fori_loop(0, 6, body, 0)

        @pl.when(i < 7)
        def _():
            forward(i + 1, 3)

        arrive(i, 3)
        lax.fori_loop(6, 8, body, 0)

        @pl.when(i < 4)
        def _():
            for cell in range(2):
                for f in range(EA):
                    outer, inner = place[f]
                    lo = (cell * EA + f) * BS
                    panel[n + 4, f, cell, outer, inner] = acc[:, lo : lo + BS].astype(jnp.bfloat16)
            send(i + 4, 0)

        @pl.when(i >= 4)
        def _():
            for cell in range(2):
                for f in range(EA):
                    outer, inner = place[f]
                    lo = (cell * EA + f) * BS
                    square = panel[n, f, cell, outer, inner].astype(jnp.float32)
                    stage[slot, cell, f] = 3.0 * square - 2.0 * acc[:, lo : lo + BS]
            out_mate(slot).start()
            out_own(slot).start()

        return 0

    lax.fori_loop(0, 2 * ITEMS, item, 0)

    for m in range(ITEMS, 2 * ITEMS):
        take(ring_send.at[m], 60, sending=True)
    out_own(ITEMS - 1).wait()
    out_mate(ITEMS - 1).wait_send()
    out_arrival(ITEMS - 1).wait_recv()


def shards(density, band_length, band_start):
    dma = pltpu.SemaphoreType.DMA
    result = pl.pallas_call(
        purify,
        out_shape=jax.ShapeDtypeStruct((2 * ITEMS, EA, BS, BS), jnp.float32),
        in_specs=[
            pl.BlockSpec(memory_space=pltpu.HBM),
            pl.BlockSpec(memory_space=pltpu.HBM),
            pl.BlockSpec(memory_space=pltpu.HBM),
            pl.BlockSpec(memory_space=pltpu.HBM),
        ],
        out_specs=pl.BlockSpec(memory_space=pl.ANY),
        scratch_shapes=[
            pltpu.VMEM((2, BANK, EA, BS, BS), jnp.bfloat16),
            pltpu.VMEM((2 * ITEMS, 2, EA, 4, 4, BS, BS), jnp.bfloat16),
            pltpu.VMEM((BS, 4 * BS), jnp.float32),
            pltpu.VMEM((ITEMS, 2, EA, BS, BS), jnp.float32),
            pltpu.SMEM((NB,), jnp.int32), pltpu.SMEM((NB,), jnp.int32), dma((2,)),
            dma((2,)), dma((2, 2)), dma((2 * ITEMS,)), dma((2 * ITEMS, 4)),
            dma((2,)), dma((2, 2)), dma((2, 2)),
            dma((3,)), dma((3,)), dma((3,)),
            dma((2, 2)), dma((2, 2)),
            dma((ITEMS,)), dma((ITEMS,)), dma((ITEMS,)),
        ],
        compiler_params=pltpu.CompilerParams(
            collective_id=0, has_side_effects=True, vmem_limit_bytes=48 * 2**20
        ),
        name="purify",
    )(
        density.reshape(SPAN, EA, BS, BS),
        density.reshape(SPAN // STRIDE, STRIDE, EA, BS, BS),
        band_length,
        band_start,
    )
    return result.reshape(2 * ITEMS, 1, 1, EA, BS, BS)


def solution(mesh):
    in_specs = (P("row", "col", "layer", None, None, None), P(), P())
    out_specs = P("row", "col", "layer", None, None, None)
    return jax.shard_map(shards, mesh=mesh, in_specs=in_specs, out_specs=out_specs, check_vma=False)
```

```python
import jax
import jax.numpy as jnp
from jax import lax
from jax.experimental import pallas as pl
from jax.experimental.pallas import tpu as pltpu
from jax.sharding import PartitionSpec as P

BS = 128
NB = 1280
SPAN = 160
STRIDE = 20
EA = 2
CELLS = 32
ITEMS = 4
BANK = 124
HALO = 22
MESH = pl.DeviceIdType.MESH


def wrap4(v):
    return lax.rem(v + 8, 4)


def purify(
    rows, density, runs_in, out,
    bank, panel, acc, stage, runs, runs_sem,
    first_send, first_recv, ring_send, ring_recv, own_sem, mate_send, mate_recv,
    bank_sem, bank_send, bank_recv, halo_send, halo_recv,
    out_sem, out_send, out_recv,
):
    z = lax.axis_index("row")
    col = lax.axis_index("col")
    x = lax.axis_index("layer")
    y = col // 2
    h = lax.rem(col, 2)
    p = 1 - h

    def at(dx=0, dy=0):
        return (z, wrap4(y + dy) * 2 + h, wrap4(x + dx))

    mate = (z, y * 2 + p, x)
    up = lax.rem(z + 1, 8)
    down = lax.rem(z + 7, 8)
    source_z = lax.rem(z + 7 + 2 * h, 8)
    barrier = pltpu.get_barrier_semaphore()
    for other in (
        at(dx=1), at(dx=-1), at(dy=1), at(dy=-1), mate,
        (source_z, y * 2, x), (source_z, y * 2 + 1, x),
    ):
        pl.semaphore_signal(barrier, inc=1, device_id=other, device_id_type=MESH)
    pl.semaphore_wait(barrier, 7)

    def local_of(i, core):
        return 3 - 3 * core + i * (2 * core - 1)

    def panel_of(i):
        slot = lax.rem(i, ITEMS)
        return i - slot + local_of(slot, h)

    def blocks_of(count):
        return bank.at[0, pl.ds(0, count // EA)]

    def take(sem, count, sending=False):
        here = blocks_of(count)
        copy = pltpu.make_async_remote_copy(
            src_ref=here, dst_ref=here, send_sem=sem, recv_sem=sem,
            device_id=mate, device_id_type=MESH,
        )
        if sending:
            copy.wait_send()
        else:
            copy.wait_recv()

    def half_of(half, core):
        return 2 - 2 * core + half * (4 * core - 2)

    def own_copy(g):
        return pltpu.make_async_copy(
            density.at[pl.ds(4 * h, 4), STRIDE // 2, g],
            panel.at[pl.ds(0, 4), g, h, 0, 0],
            own_sem.at[g],
        )

    def mate_copy(half, g):
        low = half_of(half, p)
        return pltpu.make_async_remote_copy(
            src_ref=density.at[pl.ds(4 * p + low, 2), STRIDE // 2, g],
            dst_ref=panel.at[pl.ds(low, 2), g, h, 0, 0],
            send_sem=mate_send.at[half, g],
            recv_sem=mate_recv.at[half, g],
            device_id=mate,
            device_id_type=MESH,
        )

    def mate_arrival(half, g):
        here = panel.at[pl.ds(half_of(half, h), 2), g, p, 0, 0]
        return pltpu.make_async_remote_copy(
            src_ref=here, dst_ref=here,
            send_sem=mate_send.at[half, g], recv_sem=mate_recv.at[half, g],
            device_id=mate, device_id_type=MESH,
        )

    def target(g, step, way):
        move = 1 - 2 * way
        if (g == 0) == (step < 2):
            return at(dx=move)
        return at(dy=move)

    def push(src, dst, send_sem, recv_sem, g, step, way):
        pltpu.make_async_remote_copy(
            src_ref=src, dst_ref=dst, send_sem=send_sem, recv_sem=recv_sem,
            device_id=target(g, step, way), device_id_type=MESH,
        ).start()

    near = (1, 3)

    def first_own(half):
        low = half_of(half, h)
        for g in range(2):
            for way in range(2):
                push(
                    density.at[pl.ds(4 * h + low, 2), STRIDE // 2, g],
                    panel.at[pl.ds(low, 2), g, h, 0, near[way]],
                    first_send.at[half], first_recv.at[half, 0], g, 0, way,
                )

    def first_mate(half):
        windows = pl.ds(half_of(half, h), 2)
        for g in range(2):
            mate_arrival(half, g).wait_recv()
            for way in range(2):
                push(
                    panel.at[windows, g, p, 0, 0],
                    panel.at[windows, g, p, 0, near[way]],
                    first_send.at[half], first_recv.at[half, 0], g, 0, way,
                )

    def first_both(half):
        windows = pl.ds(half_of(half, h), 2)
        for g in range(2):
            mate_arrival(half, g).wait_recv()
            for way in range(2):
                push(
                    panel.at[windows, g, :, 0, 0],
                    panel.at[windows, g, :, 0, near[way]],
                    first_send.at[half], first_recv.at[half, 0], g, 0, way,
                )

    def first_across(half):
        windows = pl.ds(half_of(half, h), 2)
        for g in range(2):
            for way in range(2):
                push(
                    panel.at[windows, g, :, 0, 0],
                    panel.at[windows, g, :, near[way], 0],
                    first_send.at[half], first_recv.at[half, 2], g, 2, way,
                )

    def first_forward(half):
        windows = pl.ds(half_of(half, h), 2)
        take(first_recv.at[half, 0], 16)
        for g in range(2):
            for way in range(2):
                push(
                    panel.at[windows, g, way, 0, near[way]],
                    panel.at[windows, g, way, 0, 2],
                    first_send.at[half], first_recv.at[half, 1], g, 1, way,
                )

    def send(i, step, part=None):
        n = panel_of(i)
        for g in range(2):
            for way in range(2):
                if step == 0:
                    src = panel.at[n, g, :, 0, 0]
                    dst = panel.at[n, g, :, 0, near[way]]
                elif step == 1:
                    src = panel.at[n, g, way, 0, near[way]]
                    dst = panel.at[n, g, way, 0, 2]
                elif step == 2:
                    src = panel.at[n, g, :, 0, part]
                    dst = panel.at[n, g, :, near[way], part]
                else:
                    src = panel.at[n, g, way, near[way]]
                    dst = panel.at[n, g, way, 2]
                push(src, dst, ring_send.at[i], ring_recv.at[i, step], g, step, way)

    own_place = 0
    other_places = pl.ds(1, 3)

    for g in range(2):
        mate_copy(0, g).start()
    first_own(0)
    for g in range(2):
        own_copy(g).start()
    for g in range(2):
        mate_copy(1, g).start()
    first_mate(0)
    own_copy(0).wait()
    own_copy(1).wait()
    first_both(1)
    first_across(0)
    pltpu.make_async_copy(runs_in, runs, runs_sem).start()

    def bank_piece(piece, core):
        if piece == 0:
            return 64, 38 + 20 * core, 60 - 60 * core
        if piece == 1:
            return 20, 18 + 104 * core, 40 + 24 * core
        return 18, 142 * core, 22 + 62 * core

    def bank_own(piece):
        size, src, dst = bank_piece(piece, h)
        return pltpu.make_async_copy(
            rows.at[pl.ds(src, size)], bank.at[h, pl.ds(dst, size)], bank_sem.at[piece]
        )

    def bank_mate(piece):
        size, src, dst = bank_piece(piece, p)
        return pltpu.make_async_remote_copy(
            src_ref=rows.at[pl.ds(src, size)],
            dst_ref=bank.at[h, pl.ds(dst, size)],
            send_sem=bank_send.at[piece],
            recv_sem=bank_recv.at[piece],
            device_id=mate,
            device_id_type=MESH,
        )

    def bank_arrival(piece):
        size, _, dst = bank_piece(piece, h)
        here = bank.at[p, pl.ds(dst, size)]
        return pltpu.make_async_remote_copy(
            src_ref=here, dst_ref=here, send_sem=bank_send.at[piece], recv_sem=bank_recv.at[piece],
            device_id=mate, device_id_type=MESH,
        )

    def halo_copy(piece, side):
        size = (2, 20)[piece]
        src = ((SPAN - 2, SPAN - 22), (0, 2))[side][piece]
        dst = ((20, 0), (102, 104))[side][piece]
        return pltpu.make_async_remote_copy(
            src_ref=rows.at[pl.ds(src, size)],
            dst_ref=bank.at[h, pl.ds(dst, size)],
            send_sem=halo_send.at[piece, side],
            recv_sem=halo_recv.at[piece, h],
            device_id=((up, y * 2, x), (down, y * 2 + 1, x))[side],
            device_id_type=MESH,
        )

    def halo_arrival(piece, cell):
        size = (2, 20)[piece]
        dst = (20 + 82 * h, 104 * h)[piece]
        here = bank.at[cell, pl.ds(dst, size)]
        return pltpu.make_async_remote_copy(
            src_ref=here, dst_ref=here,
            send_sem=halo_send.at[piece, 0], recv_sem=halo_recv.at[piece, cell],
            device_id=mate, device_id_type=MESH,
        )

    for piece in range(2):
        for side in range(2):
            halo_copy(piece, side).start()
    for piece in range(3):
        bank_mate(piece).start()
        bank_own(piece).start()

    first_forward(0)
    first_forward(1)
    first_across(1)
    take(first_recv.at[0, 1], 8)
    send(0, 2, other_places)
    send(1, 2, other_places)
    take(first_recv.at[1, 1], 8)
    pltpu.make_async_copy(runs_in, runs, runs_sem).wait()
    take(first_recv.at[0, 2], 16)
    take(ring_recv.at[0, 2], 24)
    send(0, 3)
    take(first_recv.at[1, 2], 16)

    def slab(n, local, g, far):
        outer_at = wrap4(y + g * (x - y) - far)
        anchor = STRIDE // 2 + STRIDE * (4 * h + local)
        bank0 = STRIDE * local
        row0 = SPAN * z + anchor - 32
        places = [
            lax.rem(8 * x + 2 * y + cell + 256 - anchor, CELLS) for cell in range(2)
        ]
        left, right = [], []
        for inner in range(4):
            inner_at = wrap4(x + g * (y - x) - inner)
            residue = 8 * inner_at + 2 * outer_at + g * (6 * outer_at - 6 * inner_at)
            for place_cell in range(2):
                t = lax.rem(residue + place_cell + 256 - anchor, CELLS) + CELLS * g
                k = row0 + t
                k = jnp.where(k < 0, k + NB, jnp.where(k >= NB, k - NB, k))
                run_start = runs[NB + k]
                run_length = runs[k]
                pieces = []
                for cell in range(2):
                    s0 = bank[cell, bank0 + t, 0]
                    s1 = bank[cell, bank0 + t, 1]
                    for f in range(EA):
                        at_run = places[cell] + CELLS * f - t - run_start
                        live = (at_run >= 0) & (at_run < run_length)
                        code = jnp.where(live, jnp.where(at_run < CELLS, 1, 2), 0)
                        pieces.append(
                            jnp.where(code == 1, s0, jnp.where(code == 2, s1, jnp.zeros_like(s1)))
                        )
                right.append(jnp.concatenate(pieces, axis=1))
                left.append(panel[n, g, place_cell, far, inner])
        acc[...] += jnp.dot(
            jnp.concatenate(left, axis=1),
            jnp.concatenate(right, axis=0),
            preferred_element_type=jnp.float32,
        )

    def out_own(slot):
        return pltpu.make_async_copy(
            stage.at[slot, h], out.at[4 * h + local_of(slot, h)], out_sem.at[slot]
        )

    def out_mate(slot):
        return pltpu.make_async_remote_copy(
            src_ref=stage.at[slot, p],
            dst_ref=out.at[4 * h + local_of(slot, h)],
            send_sem=out_send.at[slot],
            recv_sem=out_recv.at[slot],
            device_id=mate,
            device_id_type=MESH,
        )

    def out_arrival(slot):
        here = out.at[4 * p + local_of(slot, p)]
        return pltpu.make_async_remote_copy(
            src_ref=here, dst_ref=here, send_sem=out_send.at[slot], recv_sem=out_recv.at[slot],
            device_id=mate, device_id_type=MESH,
        )

    def item(i, _):
        slot = lax.rem(i, ITEMS)
        local = local_of(slot, h)
        n = panel_of(i)

        @pl.when((i >= 2) & (i < 6))
        def _():
            take(ring_recv.at[i + 2, 1], 4)

        @pl.when(i < 6)
        def _():
            send(i + 2, 2, other_places)

        @pl.when(i == 0)
        def _():
            bank_own(0).wait()
            bank_arrival(0).wait_recv()

        @pl.when(i == 1)
        def _():
            bank_own(1).wait()
            bank_arrival(1).wait_recv()

        @pl.when(i == 2)
        def _():
            bank_own(2).wait()
            bank_arrival(2).wait_recv()
            halo_arrival(0, 0).wait_recv()
            halo_arrival(0, 1).wait_recv()

        @pl.when(i == 3)
        def _():
            halo_arrival(1, 0).wait_recv()
            halo_arrival(1, 1).wait_recv()

        @pl.when(i == 5)
        def _():
            for half in range(2):
                take(first_send.at[half], 40, sending=True)
                for g in range(2):
                    mate_copy(half, g).wait_send()
            for m in range(ITEMS):
                take(ring_send.at[m], 40, sending=True)
            for piece in range(3):
                bank_mate(piece).wait_send()
            for piece in range(2):
                for side in range(2):
                    halo_copy(piece, side).wait_send()

        acc[...] = jnp.zeros_like(acc)

        def body(j, _):
            ring = j // 2
            slab(n, local, lax.rem(j, 2), ring + ring // 2)
            return 0

        def last(g, _):
            slab(n, local, g, 2)
            return 0

        lax.fori_loop(0, 6, body, 0)

        @pl.when((i >= 1) & (i < 5))
        def _():
            take(ring_recv.at[i + 3, 0], 8)
            send(i + 3, 1)

        @pl.when(i < 3)
        def _():
            take(ring_recv.at[i + 1, 2], 24)

        @pl.when((i >= 3) & (i < 7))
        def _():
            take(ring_recv.at[i + 1, 2], 32)

        @pl.when(i < 7)
        def _():
            send(i + 1, 3)

        take(ring_recv.at[i, 3], 16)
        lax.fori_loop(0, 2, last, 0)

        @pl.when(i < 4)
        def _():
            for cell in range(2):
                for f in range(EA):
                    lo = (cell * EA + f) * BS
                    panel[n + 4, f, cell, 0, 0] = acc[:, lo : lo + BS].astype(jnp.bfloat16)
            send(i + 4, 0)
            send(i + 4, 2, own_place)

        @pl.when(i >= 4)
        def _():
            for cell in range(2):
                for f in range(EA):
                    lo = (cell * EA + f) * BS
                    square = panel[n, f, cell, 0, 0].astype(jnp.float32)
                    stage[slot, cell, f] = 3.0 * square - 2.0 * acc[:, lo : lo + BS]
            out_mate(slot).start()
            out_own(slot).start()

        return 0

    lax.fori_loop(0, 2 * ITEMS, item, 0)

    for m in range(ITEMS, 2 * ITEMS):
        take(ring_send.at[m], 60, sending=True)
    for slot in range(ITEMS):
        out_own(slot).wait()
        out_mate(slot).wait_send()
        out_arrival(slot).wait_recv()


def shards(density, band_length, band_start):
    dma = pltpu.SemaphoreType.DMA
    result = pl.pallas_call(
        purify,
        out_shape=jax.ShapeDtypeStruct((2 * ITEMS, EA, BS, BS), jnp.float32),
        in_specs=[
            pl.BlockSpec(memory_space=pl.ANY),
            pl.BlockSpec(memory_space=pl.ANY),
            pl.BlockSpec(memory_space=pl.ANY),
        ],
        out_specs=pl.BlockSpec(memory_space=pl.ANY),
        scratch_shapes=[
            pltpu.VMEM((2, BANK, EA, BS, BS), jnp.bfloat16),
            pltpu.VMEM((2 * ITEMS, 2, EA, 4, 4, BS, BS), jnp.bfloat16),
            pltpu.VMEM((BS, 4 * BS), jnp.float32),
            pltpu.VMEM((ITEMS, 2, EA, BS, BS), jnp.float32),
            pltpu.SMEM((2 * NB,), jnp.int32), dma(()),
            dma((2,)), dma((2, 3)), dma((2 * ITEMS,)), dma((2 * ITEMS, 4)),
            dma((2,)), dma((2, 2)), dma((2, 2)),
            dma((3,)), dma((3,)), dma((3,)),
            dma((2, 2)), dma((2, 2)),
            dma((ITEMS,)), dma((ITEMS,)), dma((ITEMS,)),
        ],
        compiler_params=pltpu.CompilerParams(
            collective_id=0, has_side_effects=True, vmem_limit_bytes=48 * 2**20
        ),
        name="purify",
    )(
        density.reshape(SPAN, EA, BS, BS),
        density.reshape(SPAN // STRIDE, STRIDE, EA, BS, BS),
        jnp.concatenate([band_length, band_start]),
    )
    return result.reshape(2 * ITEMS, 1, 1, EA, BS, BS)


def solution(mesh):
    in_specs = (P("row", "col", "layer", None, None, None), P(), P())
    out_specs = P("row", "col", "layer", None, None, None)
    return jax.shard_map(shards, mesh=mesh, in_specs=in_specs, out_specs=out_specs, check_vma=False)
```

```python
import jax
import jax.numpy as jnp
from jax import lax
from jax.experimental import pallas as pl
from jax.experimental.pallas import tpu as pltpu
from jax.sharding import PartitionSpec as P

BS = 128
NB = 1280
SPAN = 160
STRIDE = 20
EA = 2
CELLS = 32
ITEMS = 4
BANK = 124
HALO = 22
MESH = pl.DeviceIdType.MESH


def wrap4(v):
    return lax.rem(v + 8, 4)


def purify(
    rows, density, runs_in, out,
    bank, panel, acc, stage, runs, runs_sem,
    first_send, first_recv, ring_send, ring_recv, own_sem, mate_send, mate_recv,
    bank_sem, bank_send, bank_recv, halo_send, halo_recv,
    out_sem, out_send, out_recv,
):
    z = lax.axis_index("row")
    col = lax.axis_index("col")
    x = lax.axis_index("layer")
    y = col // 2
    h = lax.rem(col, 2)
    p = 1 - h

    def at(dx=0, dy=0):
        return (z, wrap4(y + dy) * 2 + h, wrap4(x + dx))

    mate = (z, y * 2 + p, x)
    up = lax.rem(z + 1, 8)
    down = lax.rem(z + 7, 8)
    source_z = lax.rem(z + 7 + 2 * h, 8)
    barrier = pltpu.get_barrier_semaphore()
    for other in (
        at(dx=1), at(dx=-1), at(dy=1), at(dy=-1), mate,
        (source_z, y * 2, x), (source_z, y * 2 + 1, x),
    ):
        pl.semaphore_signal(barrier, inc=1, device_id=other, device_id_type=MESH)
    pl.semaphore_wait(barrier, 7)

    def local_of(i, core):
        return 3 - 3 * core + i * (2 * core - 1)

    def panel_of(i):
        slot = lax.rem(i, ITEMS)
        return i - slot + local_of(slot, h)

    def blocks_of(count):
        return bank.at[0, pl.ds(0, count // EA)]

    def take(sem, count, sending=False):
        here = blocks_of(count)
        copy = pltpu.make_async_remote_copy(
            src_ref=here, dst_ref=here, send_sem=sem, recv_sem=sem,
            device_id=mate, device_id_type=MESH,
        )
        if sending:
            copy.wait_send()
        else:
            copy.wait_recv()

    def half_of(half, core):
        return 2 - 2 * core + half * (4 * core - 2)

    def own_copy(g):
        return pltpu.make_async_copy(
            density.at[pl.ds(4 * h, 4), STRIDE // 2, g],
            panel.at[pl.ds(0, 4), g, h, 0, 0],
            own_sem.at[g],
        )

    def mate_copy(half, g):
        low = half_of(half, p)
        return pltpu.make_async_remote_copy(
            src_ref=density.at[pl.ds(4 * p + low, 2), STRIDE // 2, g],
            dst_ref=panel.at[pl.ds(low, 2), g, h, 0, 0],
            send_sem=mate_send.at[half, g],
            recv_sem=mate_recv.at[half, g],
            device_id=mate,
            device_id_type=MESH,
        )

    def mate_arrival(half, g):
        here = panel.at[pl.ds(half_of(half, h), 2), g, p, 0, 0]
        return pltpu.make_async_remote_copy(
            src_ref=here, dst_ref=here,
            send_sem=mate_send.at[half, g], recv_sem=mate_recv.at[half, g],
            device_id=mate, device_id_type=MESH,
        )

    def target(g, step, way):
        move = 1 - 2 * way
        if (g == 0) == (step < 2):
            return at(dx=move)
        return at(dy=move)

    def push(src, dst, send_sem, recv_sem, g, step, way):
        pltpu.make_async_remote_copy(
            src_ref=src, dst_ref=dst, send_sem=send_sem, recv_sem=recv_sem,
            device_id=target(g, step, way), device_id_type=MESH,
        ).start()

    near = (1, 3)

    def first_own(half):
        low = half_of(half, h)
        for g in range(2):
            for way in range(2):
                push(
                    density.at[pl.ds(4 * h + low, 2), STRIDE // 2, g],
                    panel.at[pl.ds(low, 2), g, h, 0, near[way]],
                    first_send.at[half], first_recv.at[half, 0], g, 0, way,
                )

    def first_mate(half):
        windows = pl.ds(half_of(half, h), 2)
        for g in range(2):
            mate_arrival(half, g).wait_recv()
            for way in range(2):
                push(
                    panel.at[windows, g, p, 0, 0],
                    panel.at[windows, g, p, 0, near[way]],
                    first_send.at[half], first_recv.at[half, 0], g, 0, way,
                )

    def first_both(half):
        windows = pl.ds(half_of(half, h), 2)
        for g in range(2):
            mate_arrival(half, g).wait_recv()
            for way in range(2):
                push(
                    panel.at[windows, g, :, 0, 0],
                    panel.at[windows, g, :, 0, near[way]],
                    first_send.at[half], first_recv.at[half, 0], g, 0, way,
                )

    def first_across(half):
        windows = pl.ds(half_of(half, h), 2)
        for g in range(2):
            for way in range(2):
                push(
                    panel.at[windows, g, :, 0, 0],
                    panel.at[windows, g, :, near[way], 0],
                    first_send.at[half], first_recv.at[half, 2], g, 2, way,
                )

    def first_forward(half):
        windows = pl.ds(half_of(half, h), 2)
        take(first_recv.at[half, 0], 16)
        for g in range(2):
            for way in range(2):
                push(
                    panel.at[windows, g, way, 0, near[way]],
                    panel.at[windows, g, way, 0, 2],
                    first_send.at[half], first_recv.at[half, 1], g, 1, way,
                )

    def send(i, step, part=None):
        n = panel_of(i)
        for g in range(2):
            for way in range(2):
                if step == 0:
                    src = panel.at[n, g, :, 0, 0]
                    dst = panel.at[n, g, :, 0, near[way]]
                elif step == 1:
                    src = panel.at[n, g, way, 0, near[way]]
                    dst = panel.at[n, g, way, 0, 2]
                elif step == 2:
                    src = panel.at[n, g, :, 0, part]
                    dst = panel.at[n, g, :, near[way], part]
                else:
                    src = panel.at[n, g, way, near[way]]
                    dst = panel.at[n, g, way, 2]
                push(src, dst, ring_send.at[i], ring_recv.at[i, step], g, step, way)

    own_place = 0
    other_places = pl.ds(1, 3)

    for g in range(2):
        mate_copy(0, g).start()
    first_own(0)
    for g in range(2):
        own_copy(g).start()
    for g in range(2):
        mate_copy(1, g).start()
    first_mate(0)
    own_copy(0).wait()
    own_copy(1).wait()
    first_both(1)
    first_across(0)
    pltpu.make_async_copy(runs_in, runs, runs_sem).start()

    def bank_piece(piece, core):
        if piece == 0:
            return 64, 38 + 20 * core, 60 - 60 * core
        if piece == 1:
            return 20, 18 + 104 * core, 40 + 24 * core
        return 18, 142 * core, 22 + 62 * core

    def bank_own(piece):
        size, src, dst = bank_piece(piece, h)
        return pltpu.make_async_copy(
            rows.at[pl.ds(src, size)], bank.at[h, pl.ds(dst, size)], bank_sem.at[piece]
        )

    def bank_mate(piece):
        size, src, dst = bank_piece(piece, p)
        return pltpu.make_async_remote_copy(
            src_ref=rows.at[pl.ds(src, size)],
            dst_ref=bank.at[h, pl.ds(dst, size)],
            send_sem=bank_send.at[piece],
            recv_sem=bank_recv.at[piece],
            device_id=mate,
            device_id_type=MESH,
        )

    def bank_arrival(piece):
        size, _, dst = bank_piece(piece, h)
        here = bank.at[p, pl.ds(dst, size)]
        return pltpu.make_async_remote_copy(
            src_ref=here, dst_ref=here, send_sem=bank_send.at[piece], recv_sem=bank_recv.at[piece],
            device_id=mate, device_id_type=MESH,
        )

    def halo_copy(piece, side):
        size = (2, 20)[piece]
        src = ((SPAN - 2, SPAN - 22), (0, 2))[side][piece]
        dst = ((20, 0), (102, 104))[side][piece]
        return pltpu.make_async_remote_copy(
            src_ref=rows.at[pl.ds(src, size)],
            dst_ref=bank.at[h, pl.ds(dst, size)],
            send_sem=halo_send.at[piece, side],
            recv_sem=halo_recv.at[piece, h],
            device_id=((up, y * 2, x), (down, y * 2 + 1, x))[side],
            device_id_type=MESH,
        )

    def halo_arrival(piece, cell):
        size = (2, 20)[piece]
        dst = (20 + 82 * h, 104 * h)[piece]
        here = bank.at[cell, pl.ds(dst, size)]
        return pltpu.make_async_remote_copy(
            src_ref=here, dst_ref=here,
            send_sem=halo_send.at[piece, 0], recv_sem=halo_recv.at[piece, cell],
            device_id=mate, device_id_type=MESH,
        )

    for piece in range(2):
        for side in range(2):
            halo_copy(piece, side).start()
    for piece in range(3):
        bank_mate(piece).start()
        bank_own(piece).start()

    first_forward(0)
    first_forward(1)
    first_across(1)
    take(first_recv.at[0, 1], 8)
    send(0, 2, other_places)
    send(1, 2, other_places)
    take(first_recv.at[1, 1], 8)
    pltpu.make_async_copy(runs_in, runs, runs_sem).wait()
    take(first_recv.at[0, 2], 16)
    take(ring_recv.at[0, 2], 24)
    send(0, 3)
    take(first_recv.at[1, 2], 16)

    def slab(n, local, far):
        anchor = STRIDE // 2 + STRIDE * (4 * h + local)
        bank0 = STRIDE * local
        row0 = SPAN * z + anchor - 32
        places = [
            lax.rem(8 * x + 2 * y + cell + 256 - anchor, CELLS) for cell in range(2)
        ]
        left, right = [], []
        for g in range(2):
            outer_at = wrap4((y, x)[g] - far)
            for inner in range(4):
                inner_at = wrap4((x, y)[g] - inner)
                residue = (8, 2)[g] * inner_at + (2, 8)[g] * outer_at
                for place_cell in range(2):
                    t = lax.rem(residue + place_cell + 256 - anchor, CELLS) + CELLS * g
                    k = row0 + t
                    k = jnp.where(k < 0, k + NB, jnp.where(k >= NB, k - NB, k))
                    run_start = runs[NB + k]
                    run_length = runs[k]
                    pieces = []
                    for cell in range(2):
                        s0 = bank[cell, bank0 + t, 0]
                        s1 = bank[cell, bank0 + t, 1]
                        for f in range(EA):
                            at_run = places[cell] + CELLS * f - t - run_start
                            live = (at_run >= 0) & (at_run < run_length)
                            code = jnp.where(live, jnp.where(at_run < CELLS, 1, 2), 0)
                            pieces.append(
                                jnp.where(code == 1, s0, jnp.where(code == 2, s1, jnp.zeros_like(s1)))
                            )
                    right.append(jnp.concatenate(pieces, axis=1))
                    left.append(panel[n, g, place_cell, far, inner])
        acc[...] += jnp.dot(
            jnp.concatenate(left, axis=1),
            jnp.concatenate(right, axis=0),
            preferred_element_type=jnp.float32,
        )

    def out_own(slot):
        return pltpu.make_async_copy(
            stage.at[slot, h], out.at[4 * h + local_of(slot, h)], out_sem.at[slot]
        )

    def out_mate(slot):
        return pltpu.make_async_remote_copy(
            src_ref=stage.at[slot, p],
            dst_ref=out.at[4 * h + local_of(slot, h)],
            send_sem=out_send.at[slot],
            recv_sem=out_recv.at[slot],
            device_id=mate,
            device_id_type=MESH,
        )

    def out_arrival(slot):
        here = out.at[4 * p + local_of(slot, p)]
        return pltpu.make_async_remote_copy(
            src_ref=here, dst_ref=here, send_sem=out_send.at[slot], recv_sem=out_recv.at[slot],
            device_id=mate, device_id_type=MESH,
        )

    def item(i, _):
        slot = lax.rem(i, ITEMS)
        local = local_of(slot, h)
        n = panel_of(i)

        @pl.when((i >= 2) & (i < 6))
        def _():
            take(ring_recv.at[i + 2, 1], 4)

        @pl.when(i < 6)
        def _():
            send(i + 2, 2, other_places)

        @pl.when(i == 0)
        def _():
            bank_own(0).wait()
            bank_arrival(0).wait_recv()

        @pl.when(i == 1)
        def _():
            bank_own(1).wait()
            bank_arrival(1).wait_recv()

        @pl.when(i == 2)
        def _():
            bank_own(2).wait()
            bank_arrival(2).wait_recv()
            halo_arrival(0, 0).wait_recv()
            halo_arrival(0, 1).wait_recv()

        @pl.when(i == 3)
        def _():
            halo_arrival(1, 0).wait_recv()
            halo_arrival(1, 1).wait_recv()

        @pl.when(i == 5)
        def _():
            for half in range(2):
                take(first_send.at[half], 40, sending=True)
                for g in range(2):
                    mate_copy(half, g).wait_send()
            for m in range(ITEMS):
                take(ring_send.at[m], 40, sending=True)
            for piece in range(3):
                bank_mate(piece).wait_send()
            for piece in range(2):
                for side in range(2):
                    halo_copy(piece, side).wait_send()

        acc[...] = jnp.zeros_like(acc)

        def body(j, _):
            slab(n, local, j + j // 2)
            return 0

        lax.fori_loop(0, 3, body, 0)

        @pl.when((i >= 1) & (i < 5))
        def _():
            take(ring_recv.at[i + 3, 0], 8)
            send(i + 3, 1)

        @pl.when(i < 3)
        def _():
            take(ring_recv.at[i + 1, 2], 24)

        @pl.when((i >= 3) & (i < 7))
        def _():
            take(ring_recv.at[i + 1, 2], 32)

        @pl.when(i < 7)
        def _():
            send(i + 1, 3)

        take(ring_recv.at[i, 3], 16)
        slab(n, local, 2)

        @pl.when(i < 4)
        def _():
            for cell in range(2):
                for f in range(EA):
                    lo = (cell * EA + f) * BS
                    panel[n + 4, f, cell, 0, 0] = acc[:, lo : lo + BS].astype(jnp.bfloat16)
            send(i + 4, 0)
            send(i + 4, 2, own_place)

        @pl.when(i >= 4)
        def _():
            for cell in range(2):
                for f in range(EA):
                    lo = (cell * EA + f) * BS
                    square = panel[n, f, cell, 0, 0].astype(jnp.float32)
                    stage[slot, cell, f] = 3.0 * square - 2.0 * acc[:, lo : lo + BS]
            out_mate(slot).start()
            out_own(slot).start()

        return 0

    lax.fori_loop(0, 2 * ITEMS, item, 0)

    for m in range(ITEMS, 2 * ITEMS):
        take(ring_send.at[m], 60, sending=True)
    for slot in range(ITEMS):
        out_own(slot).wait()
        out_mate(slot).wait_send()
        out_arrival(slot).wait_recv()


def shards(density, band_length, band_start):
    dma = pltpu.SemaphoreType.DMA
    result = pl.pallas_call(
        purify,
        out_shape=jax.ShapeDtypeStruct((2 * ITEMS, EA, BS, BS), jnp.float32),
        in_specs=[
            pl.BlockSpec(memory_space=pl.ANY),
            pl.BlockSpec(memory_space=pl.ANY),
            pl.BlockSpec(memory_space=pl.ANY),
        ],
        out_specs=pl.BlockSpec(memory_space=pl.ANY),
        scratch_shapes=[
            pltpu.VMEM((2, BANK, EA, BS, BS), jnp.bfloat16),
            pltpu.VMEM((2 * ITEMS, 2, EA, 4, 4, BS, BS), jnp.bfloat16),
            pltpu.VMEM((BS, 4 * BS), jnp.float32),
            pltpu.VMEM((ITEMS, 2, EA, BS, BS), jnp.float32),
            pltpu.SMEM((2 * NB,), jnp.int32), dma(()),
            dma((2,)), dma((2, 3)), dma((2 * ITEMS,)), dma((2 * ITEMS, 4)),
            dma((2,)), dma((2, 2)), dma((2, 2)),
            dma((3,)), dma((3,)), dma((3,)),
            dma((2, 2)), dma((2, 2)),
            dma((ITEMS,)), dma((ITEMS,)), dma((ITEMS,)),
        ],
        compiler_params=pltpu.CompilerParams(
            collective_id=0, has_side_effects=True, vmem_limit_bytes=48 * 2**20
        ),
        name="purify",
    )(
        density.reshape(SPAN, EA, BS, BS),
        density.reshape(SPAN // STRIDE, STRIDE, EA, BS, BS),
        jnp.concatenate([band_length, band_start]),
    )
    return result.reshape(2 * ITEMS, 1, 1, EA, BS, BS)


def solution(mesh):
    in_specs = (P("row", "col", "layer", None, None, None), P(), P())
    out_specs = P("row", "col", "layer", None, None, None)
    return jax.shard_map(shards, mesh=mesh, in_specs=in_specs, out_specs=out_specs, check_vma=False)
```

```python
import jax
import jax.numpy as jnp
from jax import lax
from jax.experimental import pallas as pl
from jax.experimental.pallas import tpu as pltpu
from jax.sharding import PartitionSpec as P

BS = 128
NB = 1280
SPAN = 160
STRIDE = 20
EA = 2
CELLS = 32
ITEMS = 4
BANK = 124
HALO = 22
MESH = pl.DeviceIdType.MESH


def wrap4(v):
    return lax.rem(v + 8, 4)


def purify(
    rows, density, runs_in, out,
    bank, panel, acc, stage, runs, runs_sem,
    first_send, first_recv, ring_send, ring_recv, own_sem, mate_send, mate_recv,
    bank_sem, bank_send, bank_recv, halo_send, halo_recv,
    out_sem, out_send, out_recv,
):
    z = lax.axis_index("row")
    col = lax.axis_index("col")
    x = lax.axis_index("layer")
    y = col // 2
    h = lax.rem(col, 2)
    p = 1 - h

    def at(dx=0, dy=0):
        return (z, wrap4(y + dy) * 2 + h, wrap4(x + dx))

    mate = (z, y * 2 + p, x)
    up = lax.rem(z + 1, 8)
    down = lax.rem(z + 7, 8)
    source_z = lax.rem(z + 7 + 2 * h, 8)
    barrier = pltpu.get_barrier_semaphore()
    for other in (
        at(dx=1), at(dx=-1), at(dy=1), at(dy=-1), mate,
        (source_z, y * 2, x), (source_z, y * 2 + 1, x),
    ):
        pl.semaphore_signal(barrier, inc=1, device_id=other, device_id_type=MESH)
    pl.semaphore_wait(barrier, 7)

    def local_of(i, core):
        return 3 - 3 * core + i * (2 * core - 1)

    def panel_of(i):
        slot = lax.rem(i, ITEMS)
        return i - slot + local_of(slot, h)

    def blocks_of(count):
        return bank.at[0, pl.ds(0, count // EA)]

    def take(sem, count, sending=False):
        here = blocks_of(count)
        copy = pltpu.make_async_remote_copy(
            src_ref=here, dst_ref=here, send_sem=sem, recv_sem=sem,
            device_id=mate, device_id_type=MESH,
        )
        if sending:
            copy.wait_send()
        else:
            copy.wait_recv()

    def half_of(half, core):
        return 2 - 2 * core + half * (4 * core - 2)

    def own_copy(g):
        return pltpu.make_async_copy(
            density.at[pl.ds(4 * h, 4), STRIDE // 2, g],
            panel.at[pl.ds(0, 4), g, h, 0, 0],
            own_sem.at[g],
        )

    def mate_copy(half, g):
        low = half_of(half, p)
        return pltpu.make_async_remote_copy(
            src_ref=density.at[pl.ds(4 * p + low, 2), STRIDE // 2, g],
            dst_ref=panel.at[pl.ds(low, 2), g, h, 0, 0],
            send_sem=mate_send.at[half, g],
            recv_sem=mate_recv.at[half, g],
            device_id=mate,
            device_id_type=MESH,
        )

    def mate_arrival(half, g):
        here = panel.at[pl.ds(half_of(half, h), 2), g, p, 0, 0]
        return pltpu.make_async_remote_copy(
            src_ref=here, dst_ref=here,
            send_sem=mate_send.at[half, g], recv_sem=mate_recv.at[half, g],
            device_id=mate, device_id_type=MESH,
        )

    def target(g, step, way):
        move = 1 - 2 * way
        if (g == 0) == (step < 2):
            return at(dx=move)
        return at(dy=move)

    def push(src, dst, send_sem, recv_sem, g, step, way):
        pltpu.make_async_remote_copy(
            src_ref=src, dst_ref=dst, send_sem=send_sem, recv_sem=recv_sem,
            device_id=target(g, step, way), device_id_type=MESH,
        ).start()

    near = (1, 3)

    def first_own(half):
        low = half_of(half, h)
        for g in range(2):
            for way in range(2):
                push(
                    density.at[pl.ds(4 * h + low, 2), STRIDE // 2, g],
                    panel.at[pl.ds(low, 2), g, h, 0, near[way]],
                    first_send.at[half], first_recv.at[half, 0], g, 0, way,
                )

    def first_mate(half):
        windows = pl.ds(half_of(half, h), 2)
        for g in range(2):
            mate_arrival(half, g).wait_recv()
            for way in range(2):
                push(
                    panel.at[windows, g, p, 0, 0],
                    panel.at[windows, g, p, 0, near[way]],
                    first_send.at[half], first_recv.at[half, 0], g, 0, way,
                )

    def first_across(half):
        windows = pl.ds(half_of(half, h), 2)
        for g in range(2):
            for way in range(2):
                push(
                    panel.at[windows, g, :, 0, 0],
                    panel.at[windows, g, :, near[way], 0],
                    first_send.at[half], first_recv.at[half, 2], g, 2, way,
                )

    def first_forward(half):
        windows = pl.ds(half_of(half, h), 2)
        take(first_recv.at[half, 0], 16)
        for g in range(2):
            for way in range(2):
                push(
                    panel.at[windows, g, way, 0, near[way]],
                    panel.at[windows, g, way, 0, 2],
                    first_send.at[half], first_recv.at[half, 1], g, 1, way,
                )

    def send(i, step, part=None):
        n = panel_of(i)
        for g in range(2):
            for way in range(2):
                if step == 0:
                    src = panel.at[n, g, :, 0, 0]
                    dst = panel.at[n, g, :, 0, near[way]]
                elif step == 1:
                    src = panel.at[n, g, way, 0, near[way]]
                    dst = panel.at[n, g, way, 0, 2]
                elif step == 2:
                    src = panel.at[n, g, :, 0, part]
                    dst = panel.at[n, g, :, near[way], part]
                else:
                    src = panel.at[n, g, way, near[way]]
                    dst = panel.at[n, g, way, 2]
                push(src, dst, ring_send.at[i], ring_recv.at[i, step], g, step, way)

    own_place = 0
    other_places = pl.ds(1, 3)

    first_own(0)
    for half in range(2):
        for g in range(2):
            mate_copy(half, g).start()
    first_own(1)
    for g in range(2):
        own_copy(g).start()
    first_mate(0)
    own_copy(0).wait()
    own_copy(1).wait()
    first_mate(1)
    first_across(0)
    pltpu.make_async_copy(runs_in, runs, runs_sem).start()

    def bank_piece(piece, core):
        if piece == 0:
            return 64, 38 + 20 * core, 60 - 60 * core
        if piece == 1:
            return 20, 18 + 104 * core, 40 + 24 * core
        return 18, 142 * core, 22 + 62 * core

    def bank_own(piece):
        size, src, dst = bank_piece(piece, h)
        return pltpu.make_async_copy(
            rows.at[pl.ds(src, size)], bank.at[h, pl.ds(dst, size)], bank_sem.at[piece]
        )

    def bank_mate(piece):
        size, src, dst = bank_piece(piece, p)
        return pltpu.make_async_remote_copy(
            src_ref=rows.at[pl.ds(src, size)],
            dst_ref=bank.at[h, pl.ds(dst, size)],
            send_sem=bank_send.at[piece],
            recv_sem=bank_recv.at[piece],
            device_id=mate,
            device_id_type=MESH,
        )

    def bank_arrival(piece):
        size, _, dst = bank_piece(piece, h)
        here = bank.at[p, pl.ds(dst, size)]
        return pltpu.make_async_remote_copy(
            src_ref=here, dst_ref=here, send_sem=bank_send.at[piece], recv_sem=bank_recv.at[piece],
            device_id=mate, device_id_type=MESH,
        )

    def halo_copy(piece, side):
        size = (2, 20)[piece]
        src = ((SPAN - 2, SPAN - 22), (0, 2))[side][piece]
        dst = ((20, 0), (102, 104))[side][piece]
        return pltpu.make_async_remote_copy(
            src_ref=rows.at[pl.ds(src, size)],
            dst_ref=bank.at[h, pl.ds(dst, size)],
            send_sem=halo_send.at[piece, side],
            recv_sem=halo_recv.at[piece, h],
            device_id=((up, y * 2, x), (down, y * 2 + 1, x))[side],
            device_id_type=MESH,
        )

    def halo_arrival(piece, cell):
        size = (2, 20)[piece]
        dst = (20 + 82 * h, 104 * h)[piece]
        here = bank.at[cell, pl.ds(dst, size)]
        return pltpu.make_async_remote_copy(
            src_ref=here, dst_ref=here,
            send_sem=halo_send.at[piece, 0], recv_sem=halo_recv.at[piece, cell],
            device_id=mate, device_id_type=MESH,
        )

    for piece in range(2):
        for side in range(2):
            halo_copy(piece, side).start()
    for piece in range(3):
        bank_mate(piece).start()
        bank_own(piece).start()

    first_forward(0)
    first_forward(1)
    first_across(1)
    take(first_recv.at[0, 1], 8)
    send(0, 2, other_places)
    send(1, 2, other_places)
    take(first_recv.at[1, 1], 8)
    pltpu.make_async_copy(runs_in, runs, runs_sem).wait()
    take(first_recv.at[0, 2], 16)
    take(ring_recv.at[0, 2], 24)
    send(0, 3)
    take(first_recv.at[1, 2], 16)

    def slab(n, local, far):
        anchor = STRIDE // 2 + STRIDE * (4 * h + local)
        bank0 = STRIDE * local
        row0 = SPAN * z + anchor - 32
        places = [
            lax.rem(8 * x + 2 * y + cell + 256 - anchor, CELLS) for cell in range(2)
        ]
        left, right = [], []
        for g in range(2):
            outer_at = wrap4((y, x)[g] - far)
            for inner in range(4):
                inner_at = wrap4((x, y)[g] - inner)
                residue = (8, 2)[g] * inner_at + (2, 8)[g] * outer_at
                for place_cell in range(2):
                    t = lax.rem(residue + place_cell + 256 - anchor, CELLS) + CELLS * g
                    k = row0 + t
                    k = jnp.where(k < 0, k + NB, jnp.where(k >= NB, k - NB, k))
                    run_start = runs[NB + k]
                    run_length = runs[k]
                    pieces = []
                    for cell in range(2):
                        s0 = bank[cell, bank0 + t, 0]
                        s1 = bank[cell, bank0 + t, 1]
                        for f in range(EA):
                            at_run = places[cell] + CELLS * f - t - run_start
                            live = (at_run >= 0) & (at_run < run_length)
                            code = jnp.where(live, jnp.where(at_run < CELLS, 1, 2), 0)
                            pieces.append(
                                jnp.where(code == 1, s0, jnp.where(code == 2, s1, jnp.zeros_like(s1)))
                            )
                    right.append(jnp.concatenate(pieces, axis=1))
                    left.append(panel[n, g, place_cell, far, inner])
        part = jnp.dot(
            jnp.concatenate(left, axis=1),
            jnp.concatenate(right, axis=0),
            preferred_element_type=jnp.float32,
        )
        if far == 0:
            acc[...] = part
        else:
            acc[...] += part

    def out_own(slot):
        return pltpu.make_async_copy(
            stage.at[slot, h], out.at[4 * h + local_of(slot, h)], out_sem.at[slot]
        )

    def out_mate(slot):
        return pltpu.make_async_remote_copy(
            src_ref=stage.at[slot, p],
            dst_ref=out.at[4 * h + local_of(slot, h)],
            send_sem=out_send.at[slot],
            recv_sem=out_recv.at[slot],
            device_id=mate,
            device_id_type=MESH,
        )

    def out_arrival(slot):
        here = out.at[4 * p + local_of(slot, p)]
        return pltpu.make_async_remote_copy(
            src_ref=here, dst_ref=here, send_sem=out_send.at[slot], recv_sem=out_recv.at[slot],
            device_id=mate, device_id_type=MESH,
        )

    def item(i, _):
        slot = lax.rem(i, ITEMS)
        local = local_of(slot, h)
        n = panel_of(i)

        @pl.when((i >= 2) & (i < 6))
        def _():
            take(ring_recv.at[i + 2, 1], 4)

        @pl.when(i < 6)
        def _():
            send(i + 2, 2, other_places)

        @pl.when(i == 0)
        def _():
            bank_own(0).wait()
            bank_arrival(0).wait_recv()

        @pl.when(i == 1)
        def _():
            bank_own(1).wait()
            bank_arrival(1).wait_recv()

        @pl.when(i == 2)
        def _():
            bank_own(2).wait()
            bank_arrival(2).wait_recv()
            halo_arrival(0, 0).wait_recv()
            halo_arrival(0, 1).wait_recv()

        @pl.when(i == 3)
        def _():
            halo_arrival(1, 0).wait_recv()
            halo_arrival(1, 1).wait_recv()

        @pl.when(i == 5)
        def _():
            for half in range(2):
                take(first_send.at[half], 40, sending=True)
                for g in range(2):
                    mate_copy(half, g).wait_send()
            for m in range(ITEMS):
                take(ring_send.at[m], 40, sending=True)
            for piece in range(3):
                bank_mate(piece).wait_send()
            for piece in range(2):
                for side in range(2):
                    halo_copy(piece, side).wait_send()

        for far in (0, 1, 3):
            slab(n, local, far)

        @pl.when((i >= 1) & (i < 5))
        def _():
            take(ring_recv.at[i + 3, 0], 8)
            send(i + 3, 1)

        @pl.when(i < 3)
        def _():
            take(ring_recv.at[i + 1, 2], 24)

        @pl.when((i >= 3) & (i < 7))
        def _():
            take(ring_recv.at[i + 1, 2], 32)

        @pl.when(i < 7)
        def _():
            send(i + 1, 3)

        take(ring_recv.at[i, 3], 16)
        slab(n, local, 2)

        @pl.when(i < 4)
        def _():
            for cell in range(2):
                for f in range(EA):
                    lo = (cell * EA + f) * BS
                    panel[n + 4, f, cell, 0, 0] = acc[:, lo : lo + BS].astype(jnp.bfloat16)
            send(i + 4, 0)
            send(i + 4, 2, own_place)

        @pl.when(i >= 4)
        def _():
            for cell in range(2):
                for f in range(EA):
                    lo = (cell * EA + f) * BS
                    square = panel[n, f, cell, 0, 0].astype(jnp.float32)
                    stage[slot, cell, f] = 3.0 * square - 2.0 * acc[:, lo : lo + BS]
            out_mate(slot).start()
            out_own(slot).start()

        return 0

    lax.fori_loop(0, 2 * ITEMS, item, 0)

    for m in range(ITEMS, 2 * ITEMS):
        take(ring_send.at[m], 60, sending=True)
    for slot in range(ITEMS):
        out_own(slot).wait()
        out_mate(slot).wait_send()
        out_arrival(slot).wait_recv()


def shards(density, band_length, band_start):
    dma = pltpu.SemaphoreType.DMA
    result = pl.pallas_call(
        purify,
        out_shape=jax.ShapeDtypeStruct((2 * ITEMS, EA, BS, BS), jnp.float32),
        in_specs=[
            pl.BlockSpec(memory_space=pl.ANY),
            pl.BlockSpec(memory_space=pl.ANY),
            pl.BlockSpec(memory_space=pl.ANY),
        ],
        out_specs=pl.BlockSpec(memory_space=pl.ANY),
        scratch_shapes=[
            pltpu.VMEM((2, BANK, EA, BS, BS), jnp.bfloat16),
            pltpu.VMEM((2 * ITEMS, 2, EA, 4, 4, BS, BS), jnp.bfloat16),
            pltpu.VMEM((BS, 4 * BS), jnp.float32),
            pltpu.VMEM((ITEMS, 2, EA, BS, BS), jnp.float32),
            pltpu.SMEM((2 * NB,), jnp.int32), dma(()),
            dma((2,)), dma((2, 3)), dma((2 * ITEMS,)), dma((2 * ITEMS, 4)),
            dma((2,)), dma((2, 2)), dma((2, 2)),
            dma((3,)), dma((3,)), dma((3,)),
            dma((2, 2)), dma((2, 2)),
            dma((ITEMS,)), dma((ITEMS,)), dma((ITEMS,)),
        ],
        compiler_params=pltpu.CompilerParams(
            collective_id=0, has_side_effects=True, vmem_limit_bytes=48 * 2**20
        ),
        name="purify",
    )(
        density.reshape(SPAN, EA, BS, BS),
        density.reshape(SPAN // STRIDE, STRIDE, EA, BS, BS),
        jnp.concatenate([band_length, band_start]),
    )
    return result.reshape(2 * ITEMS, 1, 1, EA, BS, BS)


def solution(mesh):
    in_specs = (P("row", "col", "layer", None, None, None), P(), P())
    out_specs = P("row", "col", "layer", None, None, None)
    return jax.shard_map(shards, mesh=mesh, in_specs=in_specs, out_specs=out_specs, check_vma=False)
```

```python
import jax
import jax.numpy as jnp
from jax import lax
from jax.experimental import pallas as pl
from jax.experimental.pallas import tpu as pltpu
from jax.sharding import PartitionSpec as P

BS = 128
NB = 1280
SPAN = 160
STRIDE = 20
EA = 2
CELLS = 32
ITEMS = 4
BANK = 124
HALO = 22
MESH = pl.DeviceIdType.MESH


def wrap4(v):
    return lax.rem(v + 8, 4)


def purify(
    rows, density, runs_in, out,
    bank, panel, acc, stage, runs, runs_sem,
    first_send, first_recv, ring_send, ring_recv, own_sem, mate_send, mate_recv,
    bank_sem, bank_send, bank_recv, halo_send, halo_recv,
    out_sem, out_send, out_recv,
):
    z = lax.axis_index("row")
    col = lax.axis_index("col")
    x = lax.axis_index("layer")
    y = col // 2
    h = lax.rem(col, 2)
    p = 1 - h

    def at(dx=0, dy=0):
        return (z, wrap4(y + dy) * 2 + h, wrap4(x + dx))

    mate = (z, y * 2 + p, x)
    up = lax.rem(z + 1, 8)
    down = lax.rem(z + 7, 8)
    source_z = lax.rem(z + 7 + 2 * h, 8)
    barrier = pltpu.get_barrier_semaphore()
    for other in (
        at(dx=1), at(dx=-1), at(dy=1), at(dy=-1), mate,
        (source_z, y * 2, x), (source_z, y * 2 + 1, x),
    ):
        pl.semaphore_signal(barrier, inc=1, device_id=other, device_id_type=MESH)
    pl.semaphore_wait(barrier, 7)

    def local_of(i, core):
        return 3 - 3 * core + i * (2 * core - 1)

    def panel_of(i):
        slot = lax.rem(i, ITEMS)
        return i - slot + local_of(slot, h)

    def blocks_of(count):
        return bank.at[0, pl.ds(0, count // EA)]

    def take(sem, count, sending=False):
        here = blocks_of(count)
        copy = pltpu.make_async_remote_copy(
            src_ref=here, dst_ref=here, send_sem=sem, recv_sem=sem,
            device_id=mate, device_id_type=MESH,
        )
        if sending:
            copy.wait_send()
        else:
            copy.wait_recv()

    def half_of(half, core):
        return 2 - 2 * core + half * (4 * core - 2)

    def own_copy(g):
        return pltpu.make_async_copy(
            density.at[pl.ds(4 * h, 4), STRIDE // 2, g],
            panel.at[pl.ds(0, 4), g, h, 0, 0],
            own_sem.at[g],
        )

    def mate_copy(half, g):
        low = half_of(half, p)
        return pltpu.make_async_remote_copy(
            src_ref=density.at[pl.ds(4 * p + low, 2), STRIDE // 2, g],
            dst_ref=panel.at[pl.ds(low, 2), g, h, 0, 0],
            send_sem=mate_send.at[half, g],
            recv_sem=mate_recv.at[half, g],
            device_id=mate,
            device_id_type=MESH,
        )

    def mate_arrival(half, g):
        here = panel.at[pl.ds(half_of(half, h), 2), g, p, 0, 0]
        return pltpu.make_async_remote_copy(
            src_ref=here, dst_ref=here,
            send_sem=mate_send.at[half, g], recv_sem=mate_recv.at[half, g],
            device_id=mate, device_id_type=MESH,
        )

    def target(g, step, way):
        move = 1 - 2 * way
        if (g == 0) == (step < 2):
            return at(dx=move)
        return at(dy=move)

    def push(src, dst, send_sem, recv_sem, g, step, way):
        pltpu.make_async_remote_copy(
            src_ref=src, dst_ref=dst, send_sem=send_sem, recv_sem=recv_sem,
            device_id=target(g, step, way), device_id_type=MESH,
        ).start()

    near = (1, 3)

    def first_own(half):
        low = half_of(half, h)
        for g in range(2):
            for way in range(2):
                push(
                    density.at[pl.ds(4 * h + low, 2), STRIDE // 2, g],
                    panel.at[pl.ds(low, 2), g, h, 0, near[way]],
                    first_send.at[half], first_recv.at[half, 0], g, 0, way,
                )

    def first_mate(half):
        windows = pl.ds(half_of(half, h), 2)
        for g in range(2):
            mate_arrival(half, g).wait_recv()
            for way in range(2):
                push(
                    panel.at[windows, g, p, 0, 0],
                    panel.at[windows, g, p, 0, near[way]],
                    first_send.at[half], first_recv.at[half, 0], g, 0, way,
                )

    def first_across(half):
        windows = pl.ds(half_of(half, h), 2)
        for g in range(2):
            for way in range(2):
                push(
                    panel.at[windows, g, :, 0, 0],
                    panel.at[windows, g, :, near[way], 0],
                    first_send.at[half], first_recv.at[half, 2], g, 2, way,
                )

    def first_forward(half):
        windows = pl.ds(half_of(half, h), 2)
        take(first_recv.at[half, 0], 16)
        for g in range(2):
            for way in range(2):
                push(
                    panel.at[windows, g, way, 0, near[way]],
                    panel.at[windows, g, way, 0, 2],
                    first_send.at[half], first_recv.at[half, 1], g, 1, way,
                )

    def send(i, step, part=None):
        n = panel_of(i)
        for g in range(2):
            for way in range(2):
                if step == 0:
                    src = panel.at[n, g, :, 0, 0]
                    dst = panel.at[n, g, :, 0, near[way]]
                elif step == 1:
                    src = panel.at[n, g, way, 0, near[way]]
                    dst = panel.at[n, g, way, 0, 2]
                elif step == 2:
                    src = panel.at[n, g, :, 0, part]
                    dst = panel.at[n, g, :, near[way], part]
                else:
                    src = panel.at[n, g, way, near[way]]
                    dst = panel.at[n, g, way, 2]
                push(src, dst, ring_send.at[i], ring_recv.at[i, step], g, step, way)

    own_place = 0
    other_places = pl.ds(1, 3)

    first_own(0)
    for half in range(2):
        for g in range(2):
            mate_copy(half, g).start()
    first_own(1)
    for g in range(2):
        own_copy(g).start()
    first_mate(0)
    own_copy(0).wait()
    own_copy(1).wait()
    first_mate(1)
    first_across(0)
    pltpu.make_async_copy(runs_in, runs, runs_sem).start()

    def bank_piece(piece, core):
        if piece == 0:
            return 64, 38 + 20 * core, 60 - 60 * core
        if piece == 1:
            return 20, 18 + 104 * core, 40 + 24 * core
        return 18, 142 * core, 22 + 62 * core

    def bank_own(piece):
        size, src, dst = bank_piece(piece, h)
        return pltpu.make_async_copy(
            rows.at[pl.ds(src, size)], bank.at[h, pl.ds(dst, size)], bank_sem.at[piece]
        )

    def bank_mate(piece):
        size, src, dst = bank_piece(piece, p)
        return pltpu.make_async_remote_copy(
            src_ref=rows.at[pl.ds(src, size)],
            dst_ref=bank.at[h, pl.ds(dst, size)],
            send_sem=bank_send.at[piece],
            recv_sem=bank_recv.at[piece],
            device_id=mate,
            device_id_type=MESH,
        )

    def bank_arrival(piece):
        size, _, dst = bank_piece(piece, h)
        here = bank.at[p, pl.ds(dst, size)]
        return pltpu.make_async_remote_copy(
            src_ref=here, dst_ref=here, send_sem=bank_send.at[piece], recv_sem=bank_recv.at[piece],
            device_id=mate, device_id_type=MESH,
        )

    def halo_copy(piece, side):
        size = (2, 20)[piece]
        src = ((SPAN - 2, SPAN - 22), (0, 2))[side][piece]
        dst = ((20, 0), (102, 104))[side][piece]
        return pltpu.make_async_remote_copy(
            src_ref=rows.at[pl.ds(src, size)],
            dst_ref=bank.at[h, pl.ds(dst, size)],
            send_sem=halo_send.at[piece, side],
            recv_sem=halo_recv.at[piece, h],
            device_id=((up, y * 2, x), (down, y * 2 + 1, x))[side],
            device_id_type=MESH,
        )

    def halo_arrival(piece, cell):
        size = (2, 20)[piece]
        dst = (20 + 82 * h, 104 * h)[piece]
        here = bank.at[cell, pl.ds(dst, size)]
        return pltpu.make_async_remote_copy(
            src_ref=here, dst_ref=here,
            send_sem=halo_send.at[piece, 0], recv_sem=halo_recv.at[piece, cell],
            device_id=mate, device_id_type=MESH,
        )

    for piece in range(2):
        for side in range(2):
            halo_copy(piece, side).start()
    for piece in range(3):
        bank_mate(piece).start()
        bank_own(piece).start()

    first_forward(0)
    first_forward(1)
    first_across(1)
    take(first_recv.at[0, 1], 8)
    send(0, 2, other_places)
    send(1, 2, other_places)
    take(first_recv.at[1, 1], 8)
    pltpu.make_async_copy(runs_in, runs, runs_sem).wait()
    take(first_recv.at[0, 2], 16)
    take(ring_recv.at[0, 2], 24)
    send(0, 3)
    take(first_recv.at[1, 2], 16)

    def slab(n, local, far):
        anchor = STRIDE // 2 + STRIDE * (4 * h + local)
        bank0 = STRIDE * local
        row0 = SPAN * z + anchor - 32
        places = [
            lax.rem(8 * x + 2 * y + cell + 256 - anchor, CELLS) for cell in range(2)
        ]
        left, right = [], []
        for g in range(2):
            outer_at = wrap4((y, x)[g] - far)
            for inner in range(4):
                inner_at = wrap4((x, y)[g] - inner)
                residue = (8, 2)[g] * inner_at + (2, 8)[g] * outer_at
                for place_cell in range(2):
                    t = lax.rem(residue + place_cell + 256 - anchor, CELLS) + CELLS * g
                    k = row0 + t
                    k = jnp.where(k < 0, k + NB, jnp.where(k >= NB, k - NB, k))
                    run_start = runs[NB + k]
                    run_length = runs[k]
                    pieces = []
                    for cell in range(2):
                        s0 = bank[cell, bank0 + t, 0]
                        s1 = bank[cell, bank0 + t, 1]
                        for f in range(EA):
                            at_run = places[cell] + CELLS * f - t - run_start
                            live = (at_run >= 0) & (at_run < run_length)
                            code = jnp.where(live, jnp.where(at_run < CELLS, 1, 2), 0)
                            pieces.append(
                                jnp.where(code == 1, s0, jnp.where(code == 2, s1, jnp.zeros_like(s1)))
                            )
                    right.append(jnp.concatenate(pieces, axis=1))
                    left.append(panel[n, g, place_cell, far, inner])
        part = jnp.dot(
            jnp.concatenate(left, axis=1),
            jnp.concatenate(right, axis=0),
            preferred_element_type=jnp.float32,
        )
        if far == 0:
            acc[...] = part
        else:
            acc[...] += part

    def out_own(slot):
        return pltpu.make_async_copy(
            stage.at[slot, h], out.at[4 * h + local_of(slot, h)], out_sem.at[slot]
        )

    def out_mate(slot):
        return pltpu.make_async_remote_copy(
            src_ref=stage.at[slot, p],
            dst_ref=out.at[4 * h + local_of(slot, h)],
            send_sem=out_send.at[slot],
            recv_sem=out_recv.at[slot],
            device_id=mate,
            device_id_type=MESH,
        )

    def out_arrival(slot):
        here = out.at[4 * p + local_of(slot, p)]
        return pltpu.make_async_remote_copy(
            src_ref=here, dst_ref=here, send_sem=out_send.at[slot], recv_sem=out_recv.at[slot],
            device_id=mate, device_id_type=MESH,
        )

    def item(i, _):
        slot = lax.rem(i, ITEMS)
        local = local_of(slot, h)
        n = panel_of(i)

        @pl.when((i >= 2) & (i < 6))
        def _():
            take(ring_recv.at[i + 2, 1], 4)

        @pl.when(i < 6)
        def _():
            send(i + 2, 2, other_places)

        @pl.when(i == 0)
        def _():
            bank_own(0).wait()
            bank_arrival(0).wait_recv()

        @pl.when(i == 1)
        def _():
            bank_own(1).wait()
            bank_arrival(1).wait_recv()

        @pl.when(i == 2)
        def _():
            bank_own(2).wait()
            bank_arrival(2).wait_recv()
            halo_arrival(0, 0).wait_recv()
            halo_arrival(0, 1).wait_recv()

        @pl.when(i == 3)
        def _():
            halo_arrival(1, 0).wait_recv()
            halo_arrival(1, 1).wait_recv()

        @pl.when(i == 5)
        def _():
            for half in range(2):
                take(first_send.at[half], 40, sending=True)
                for g in range(2):
                    mate_copy(half, g).wait_send()
            for m in range(ITEMS):
                take(ring_send.at[m], 40, sending=True)
            for piece in range(3):
                bank_mate(piece).wait_send()
            for piece in range(2):
                for side in range(2):
                    halo_copy(piece, side).wait_send()

        for far in (0, 1, 3):
            slab(n, local, far)

        @pl.when((i >= 1) & (i < 5))
        def _():
            take(ring_recv.at[i + 3, 0], 8)
            send(i + 3, 1)

        @pl.when(i < 3)
        def _():
            take(ring_recv.at[i + 1, 2], 24)

        @pl.when((i >= 3) & (i < 7))
        def _():
            take(ring_recv.at[i + 1, 2], 32)

        @pl.when(i < 7)
        def _():
            send(i + 1, 3)

        @pl.when(i == 7)
        def _():
            for m in range(ITEMS, 6):
                take(ring_send.at[m], 60, sending=True)
            for early in range(2):
                out_own(early).wait()
                out_mate(early).wait_send()
                out_arrival(early).wait_recv()

        take(ring_recv.at[i, 3], 16)
        slab(n, local, 2)

        @pl.when(i < 4)
        def _():
            for cell in range(2):
                for f in range(EA):
                    lo = (cell * EA + f) * BS
                    panel[n + 4, f, cell, 0, 0] = acc[:, lo : lo + BS].astype(jnp.bfloat16)
            send(i + 4, 0)
            send(i + 4, 2, own_place)

        def purified(cell):
            for f in range(EA):
                lanes = pl.ds(pl.multiple_of((cell * EA + f) * BS, BS), BS)
                square = panel[n, f, cell, 0, 0].astype(jnp.float32)
                stage[slot, cell, f] = 3.0 * square - 2.0 * acc[:, lanes]

        @pl.when(i >= 4)
        def _():
            purified(p)
            out_mate(slot).start()
            purified(h)
            out_own(slot).start()

        return 0

    lax.fori_loop(0, 2 * ITEMS, item, 0)

    for m in range(6, 2 * ITEMS):
        take(ring_send.at[m], 60, sending=True)
    for slot in range(2, ITEMS):
        out_own(slot).wait()
        out_mate(slot).wait_send()
        out_arrival(slot).wait_recv()


def shards(density, band_length, band_start):
    dma = pltpu.SemaphoreType.DMA
    result = pl.pallas_call(
        purify,
        out_shape=jax.ShapeDtypeStruct((2 * ITEMS, EA, BS, BS), jnp.float32),
        in_specs=[
            pl.BlockSpec(memory_space=pl.ANY),
            pl.BlockSpec(memory_space=pl.ANY),
            pl.BlockSpec(memory_space=pl.ANY),
        ],
        out_specs=pl.BlockSpec(memory_space=pl.ANY),
        scratch_shapes=[
            pltpu.VMEM((2, BANK, EA, BS, BS), jnp.bfloat16),
            pltpu.VMEM((2 * ITEMS, 2, EA, 4, 4, BS, BS), jnp.bfloat16),
            pltpu.VMEM((BS, 4 * BS), jnp.float32),
            pltpu.VMEM((ITEMS, 2, EA, BS, BS), jnp.float32),
            pltpu.SMEM((2 * NB,), jnp.int32), dma(()),
            dma((2,)), dma((2, 3)), dma((2 * ITEMS,)), dma((2 * ITEMS, 4)),
            dma((2,)), dma((2, 2)), dma((2, 2)),
            dma((3,)), dma((3,)), dma((3,)),
            dma((2, 2)), dma((2, 2)),
            dma((ITEMS,)), dma((ITEMS,)), dma((ITEMS,)),
        ],
        compiler_params=pltpu.CompilerParams(
            collective_id=0, has_side_effects=True, vmem_limit_bytes=48 * 2**20
        ),
        name="purify",
    )(
        density.reshape(SPAN, EA, BS, BS),
        density.reshape(SPAN // STRIDE, STRIDE, EA, BS, BS),
        jnp.concatenate([band_length, band_start]),
    )
    return result.reshape(2 * ITEMS, 1, 1, EA, BS, BS)


def solution(mesh):
    in_specs = (P("row", "col", "layer", None, None, None), P(), P())
    out_specs = P("row", "col", "layer", None, None, None)
    return jax.shard_map(shards, mesh=mesh, in_specs=in_specs, out_specs=out_specs, check_vma=False)
```
